32 devices in a mesh: dp: 8 (over y, x, core), tensor: 4 (over z).
Axes of the slice: x: 2, y: 2, z: 4, core: 2. Of those that a mesh axis runs over, the one named last changes fastest.
Arguments:
- cand_gate: bfloat16 [2048, 28672], P('dp', 'tensor'), may hold values from -6 to 6
- cand_up: bfloat16 [2048, 28672], P('dp', 'tensor'), may hold values from -6 to 6
- cand_dh: bfloat16 [2048, 28672], P('dp', 'tensor'), may hold values from -6 to 6
- cand_x: bfloat16 [2048, 8192], P('dp', 'tensor'), may hold values from -6 to 6
- cand_dy: bfloat16 [2048, 8192], P('dp', 'tensor'), may hold values from -6 to 6
- val_gate: bfloat16 [2048, 28672], P('dp', 'tensor'), may hold values from -6 to 6
- val_up: bfloat16 [2048, 28672], P('dp', 'tensor'), may hold values from -6 to 6
- val_dh: bfloat16 [2048, 28672], P('dp', 'tensor'), may hold values from -6 to 6
- val_x: bfloat16 [2048, 8192], P('dp', 'tensor'), may hold values from -6 to 6
- val_dy: bfloat16 [2048, 8192], P('dp', 'tensor'), may hold values from -6 to 6
- cand_lengths: int32 [8, 8], P('dp'), may hold values from 1 to 64, 256 in all within a row
- val_lengths: int32 [8, 8], replicated, may hold values from 1 to 64, 256 in all within a row
- round_owner: int32 [2], replicated, may hold values from 0 to 7
Outputs:
- scores: float32 [2, 64, 8], P(None, 'dp')
The draws below stay inside these ranges and needn't reach their ends.
Inputs may be any that keep to these rules, and one draw needn't show every extreme that they name: Each row of cand_lengths sums to 256, and its largest entry is 64. Each row of val_lengths sums to 256, and its largest entry is 64.
All inputs are finite; a program needn't handle non-finite values.
Results may differ from the reference program's by a relative error of at most 0.0042.
Values may be sent and summed in bfloat16 or wider, within the bound.
No kernel may reach another device: no remote copies, remote signals or barrier semaphores. Data moves between devices by JAX's collectives and lax.ppermute only.
A program may use at most 128 MiB of HBM per device.

```python
import math
import jax
import jax.numpy as jnp
import numpy as np
from jax import lax

D = 8192
FF = 28672
CAND_DEV = 256
VAL_DEV = 256
CSAMP = 8
VSAMP = 8
ROUNDS = 2
CAND_TOK = 2048
VAL_TOK = 2048
N_DP = 8


def shard_levels(own_key, extent, split, low, top_value):
    def one(axis_at, parts):
        draws = jax.random.uniform(jax.random.fold_in(jax.random.fold_in(own_key, 6), axis_at), (parts,), jnp.float32, low / len(split), top_value / len(split))
        return jnp.repeat(jnp.exp(draws), extent[axis_at] // parts).reshape((-1,) + (1,) * (len(extent) - axis_at - 1))

    loudness = one(*split[0])
    for cut in split[1:]:
        loudness = loudness * one(*cut)
    return loudness


def length_profile(count, total, bound, slope):
    weights = [(1 << 20) // math.isqrt(standing ** slope) + 1 for standing in range(2, count + 1)]
    spare, given = total - bound - (count - 1), [1] * (count - 1)
    while spare > 0:
        candidates = [i for i in range(count - 1) if given[i] < bound]
        mass, remaining = sum([weights[i] for i in candidates]), spare
        for i in candidates:
            extra = min(bound - given[i], max(1, remaining * weights[i] // mass), spare)
            given[i] = given[i] + extra
            spare = spare - extra
    return np.array([bound] + given)


def uneven(key, number_of, total, most, skew):
    if number_of == 2:
        one = jax.random.randint(key, (), max(1, total - most), min(most, total - 1) + 1)
        return jnp.stack([one, total - one])
    sizes = jnp.asarray(length_profile(number_of, total, most, skew), jnp.int32)
    pairs = (number_of - 1) // 2
    source_of, sink = sizes[1:1 + 2 * pairs:2], sizes[2:2 + 2 * pairs:2]
    margin = jnp.minimum(source_of - 1, most - sink)
    passed = jax.random.randint(jax.random.fold_in(key, 1), (pairs,), 0, 1 << 20) % (margin + 1)
    sizes = sizes.at[1:1 + 2 * pairs:2].set(source_of - passed).at[2:2 + 2 * pairs:2].set(sink + passed)
    return sizes[jax.random.permutation(jax.random.fold_in(key, 2), number_of)]


def centred(stream_key, dims, scale, bound, pieces=(), held_as=jnp.bfloat16):
    values = jax.random.normal(stream_key, dims, jnp.float32) * scale
    if len(pieces) > 0:
        values = shard_levels(stream_key, dims, pieces, -0.22, 0.18) * values
    return jnp.clip(values, min=-bound, max=bound).astype(held_as)


def setup_inputs(seed: int = 0) -> dict:
    key_list = jax.random.split(jax.random.key(seed), 14)
    cand_gate = centred(key_list[0], (CAND_TOK, FF), 1.0, 6.0, ((0, 8), (1, 4)))
    cand_up = centred(key_list[1], (CAND_TOK, FF), 1.0, 6.0, ((0, 8), (1, 4)))
    cand_dh = centred(key_list[2], (CAND_TOK, FF), 1.0, 6.0, ((0, 8), (1, 4)))
    cand_x = centred(key_list[3], (CAND_TOK, D), 1.0, 6.0, ((0, 8), (1, 4)))
    cand_dy = centred(key_list[4], (CAND_TOK, D), 1.0, 6.0, ((0, 8), (1, 4)))
    val_gate = centred(key_list[5], (VAL_TOK, FF), 1.0, 6.0, ((0, 8), (1, 4)))
    val_up = centred(key_list[6], (VAL_TOK, FF), 1.0, 6.0, ((0, 8), (1, 4)))
    val_dh = centred(key_list[7], (VAL_TOK, FF), 1.0, 6.0, ((0, 8), (1, 4)))
    val_x = centred(key_list[8], (VAL_TOK, D), 1.0, 6.0, ((0, 8), (1, 4)))
    val_dy = centred(key_list[9], (VAL_TOK, D), 1.0, 6.0, ((0, 8), (1, 4)))
    cand_lengths = jax.vmap(lambda own: uneven(own, CSAMP, CAND_DEV, CAND_DEV // 4, 2))(jax.random.split(key_list[10], N_DP)).reshape((N_DP, CSAMP)).astype(jnp.int32)
    val_lengths = jax.vmap(lambda own: uneven(own, VSAMP, VAL_DEV, VAL_DEV // 4, 2))(jax.random.split(key_list[11], N_DP)).reshape((N_DP, VSAMP)).astype(jnp.int32)
    round_owner = jax.random.randint(key_list[12], (ROUNDS,), 0, N_DP).astype(jnp.int32)
    return dict(cand_gate=cand_gate, cand_up=cand_up, cand_dh=cand_dh, cand_x=cand_x, cand_dy=cand_dy, val_gate=val_gate, val_up=val_up, val_dh=val_dh, val_x=val_x, val_dy=val_dy, cand_lengths=cand_lengths, val_lengths=val_lengths, round_owner=round_owner)


def derive(gate, up, grad_hidden):
    gate_f = gate.astype(jnp.float32)
    up_f = up.astype(jnp.float32)
    grad_f = grad_hidden.astype(jnp.float32)
    sigmoid_gate = jax.nn.sigmoid(gate_f)
    activated = gate_f * sigmoid_gate
    hidden = (activated * up_f).astype(jnp.bfloat16)
    grad_gate = (grad_f * up_f * sigmoid_gate * (1.0 + gate_f * (1.0 - sigmoid_gate))).astype(jnp.bfloat16)
    grad_up = (grad_f * activated).astype(jnp.bfloat16)
    return (grad_gate, grad_up, hidden)

def onehot(lengths, total):
    bounds = jnp.cumsum(lengths.astype(jnp.int32))
    position = jnp.arange(total, dtype=jnp.int32)
    segment = lax.optimization_barrier(jnp.sum((position[:, None] >= bounds[None, :]).astype(jnp.int32), axis=1))
    labels = jnp.arange(lengths.shape[0], dtype=jnp.int32)
    return (segment[:, None] == labels[None, :]).astype(jnp.float32)

def gram(left, right):
    return jnp.dot(left, right.T, preferred_element_type=jnp.float32)

def reference(cand_gate, cand_up, cand_dh, cand_x, cand_dy, val_gate, val_up, val_dh, val_x, val_dy, cand_lengths, val_lengths, round_owner):
    score_scale = 1.0 / math.sqrt(D * FF)
    blocks = (cand_gate.reshape(N_DP, CAND_DEV, FF), cand_up.reshape(N_DP, CAND_DEV, FF), cand_dh.reshape(N_DP, CAND_DEV, FF), cand_x.reshape(N_DP, CAND_DEV, D), cand_dy.reshape(N_DP, CAND_DEV, D), cand_lengths)
    results = []
    for round_index in range(ROUNDS):
        owner_index = round_owner[round_index]
        first_row = (owner_index * VAL_DEV).astype(jnp.int32)

        def pick(array):
            return lax.dynamic_slice_in_dim(array, first_row, VAL_DEV, 0)
        val_gd, val_ud, val_hidden = derive(pick(val_gate), pick(val_up), pick(val_dh))
        val_gu = jnp.concatenate([val_gd, val_ud], axis=1)
        val_xs = pick(val_x)
        val_dys = pick(val_dy)
        val_len = lax.dynamic_index_in_dim(val_lengths, owner_index.astype(jnp.int32), 0, keepdims=False)
        val_hot = onehot(val_len, VAL_DEV)
        val_count = val_len.astype(jnp.float32)

        def member(items):
            gate, up, grad_hidden, inputs, grad_out, lengths = items
            grad_gate, grad_up, hidden = derive(gate, up, grad_hidden)
            cand_gu = jnp.concatenate([grad_gate, grad_up], axis=1)
            pair = gram(inputs, val_xs) * gram(cand_gu, val_gu) + gram(hidden, val_hidden) * gram(grad_out, val_dys)
            cand_hot = onehot(lengths, CAND_DEV)
            summed = jnp.dot(cand_hot.T, pair, precision=lax.Precision.HIGHEST)
            summed = jnp.dot(summed, val_hot, precision=lax.Precision.HIGHEST)
            cand_count = lengths.astype(jnp.float32)
            return summed * score_scale / jnp.sqrt(cand_count[:, None] * val_count[None, :])
        per_member = lax.map(member, blocks)
        results.append(per_member.reshape(N_DP * CSAMP, VSAMP))
    return jnp.stack(results, axis=0)
```

```python
import functools
import math

import jax
import jax.numpy as jnp
from jax import lax
from jax.experimental import pallas as pl
from jax.experimental.pallas import tpu as pltpu
from jax.sharding import PartitionSpec as P

D = 8192
FF = 28672
ROUNDS = 2
FB = 512
W = 3 * FB
LAG = 5
VMEM = 48 * 1024 * 1024

NT = (((1,), (1,)), ((), ()))


def derive(gate, up, grad_hidden):
    gate_f = gate.astype(jnp.float32)
    up_f = up.astype(jnp.float32)
    grad_f = grad_hidden.astype(jnp.float32)
    sigmoid_gate = jax.nn.sigmoid(gate_f)
    activated = gate_f * sigmoid_gate
    hidden = (activated * up_f).astype(jnp.bfloat16)
    grad_gate = (grad_f * up_f * sigmoid_gate * (1.0 + gate_f * (1.0 - sigmoid_gate))).astype(
        jnp.bfloat16
    )
    grad_up = (grad_f * activated).astype(jnp.bfloat16)
    return (grad_gate, grad_up, hidden)


def segment_of(lengths, total):
    bounds = jnp.cumsum(lengths)
    position = jnp.arange(total, dtype=jnp.int32)
    return jnp.sum((position[:, None] >= bounds[None, :]).astype(jnp.int32), axis=1)


def segments(j, width):
    out = []
    for which in (0, 1):
        lo = max(j * W, which * width)
        hi = min((j + 1) * W, (which + 1) * width)
        if hi > lo:
            out.append((which, lo - which * width, lo - j * W, hi - lo))
    return out


def pack_body(groups, width, first, transform, gate, up, dh, x, dy, out):
    k = pl.program_id(0) + first

    @pl.when(k < groups)
    def _():
        if transform:
            a, b, c = derive(gate[...], up[...], dh[...])
        else:
            a, b, c = gate[...], up[...], dh[...]
        out[0, :, 0:FB] = a
        out[0, :, FB : 2 * FB] = b
        out[0, :, 2 * FB : 3 * FB] = c

    for j in range(-(-2 * width // W)):

        @pl.when(k == groups + j)
        def _():
            end = 0
            for which, src, dst, cols in segments(j, width):
                out[0, :, dst : dst + cols] = (x, dy)[which][:, src : src + cols]
                end = dst + cols
            if end < W:
                out[0, :, end:W] = jnp.zeros((out.shape[1], W - end), out.dtype)


def pack_kernel(groups, width, first, transform, half, *refs):
    pack_body(groups, width, first, transform, *refs)


def pack(half, rows, first, count, transform, gate, up, dh, x, dy):
    groups, width = gate.shape[1] // FB, x.shape[1]
    wide = pl.BlockSpec(
        (rows, FB), lambda k, half: (half[0], jnp.minimum(k + first, groups - 1))
    )
    flat = pl.BlockSpec((rows, width), lambda k, half: (half[0], 0))
    return pl.pallas_call(
        functools.partial(pack_kernel, groups, width, first, transform),
        grid_spec=pltpu.PrefetchScalarGridSpec(
            num_scalar_prefetch=1,
            grid=(count,),
            in_specs=[wide, wide, wide, flat, flat],
            out_specs=pl.BlockSpec((1, rows, W), lambda k, half: (k, 0, 0)),
        ),
        out_shape=jax.ShapeDtypeStruct((count, rows, W), jnp.bfloat16),
        cost_estimate=pl.CostEstimate(
            flops=20 * count * rows * W if transform else 0,
            bytes_accessed=4 * count * rows * W,
            transcendentals=count * rows * FB if transform else 0,
        ),
        compiler_params=pltpu.CompilerParams(vmem_limit_bytes=VMEM),
    )(half, gate, up, dh, x, dy)


def inject_body(t, at, groups, width, always, info, gate, up, dh, x, dy, sib, out, sem):
    rows = out.shape[0]
    start = pl.multiple_of(info[2] * rows, rows)
    first = info[0] == 0
    mine = info[1] == 1
    if t < groups:
        parts = [
            (ref.at[pl.ds(start, rows), pl.ds(t * FB, FB)], out.at[:, pl.ds(i * FB, FB)])
            for i, ref in enumerate((gate, up, dh))
        ]
    else:
        parts = [
            (
                (x, dy)[which].at[pl.ds(start, rows), pl.ds(src, cols)],
                out.at[:, pl.ds(dst, cols)],
            )
            for which, src, dst, cols in segments(t - groups, width)
        ]

    @pl.when(mine if always else jnp.logical_and(first, mine))
    def _():
        copies = [pltpu.make_async_copy(a, b, sem.at[i]) for i, (a, b) in enumerate(parts)]
        for copy in copies:
            copy.start()
        for copy in copies:
            copy.wait()

    other = jnp.logical_not(mine)

    @pl.when(other if always else jnp.logical_and(first, other))
    def _():
        copy = pltpu.make_async_copy(sib.at[at], out, sem.at[0])
        copy.start()
        copy.wait()


def inject_first(t, at, groups, width, info, gate, up, dh, x, dy, sib, out, sem):
    inject_body(t, at, groups, width, True, info, gate, up, dh, x, dy, sib, out, sem)


def inject_later(t, at, groups, width, info, gate, up, dh, x, dy, sib, held, out, sem):
    inject_body(t, at, groups, width, False, info, gate, up, dh, x, dy, sib, out, sem)


def inject(t, at, rows, info, gate, up, dh, x, dy, sib, held):
    groups, width = gate.shape[1] // FB, x.shape[1]
    body = inject_first if held is None else inject_later
    anywhere = pl.BlockSpec(memory_space=pl.ANY)
    ins = [gate, up, dh, x, dy, sib] + ([] if held is None else [held])
    return pl.pallas_call(
        functools.partial(body, t, at, groups, width),
        in_specs=[pl.BlockSpec(memory_space=pltpu.SMEM)] + [anywhere] * len(ins),
        out_specs=anywhere,
        out_shape=jax.ShapeDtypeStruct((rows, W), jnp.bfloat16),
        scratch_shapes=[pltpu.SemaphoreType.DMA((3,))],
        input_output_aliases={} if held is None else {7: 0},
        cost_estimate=pl.CostEstimate(
            flops=0, bytes_accessed=4 * rows * W, transcendentals=0
        ),
    )(info, *ins)


def use_body(groups, width, info, val, own, sib, acc_in, acc):
    k = info[0]
    acc[...] = acc_in[...]
    rows = own.shape[1]

    def add(slot, side, cols, right):
        left = (own, sib)[side][0, :, cols]
        acc[0, slot, side * rows : (side + 1) * rows, :] += lax.dot_general(
            left, right, NT, preferred_element_type=jnp.float32
        )

    @pl.when(jnp.logical_and(k >= 0, k < groups))
    def _():
        gd, ud, hidden = derive(val[:, 0:FB], val[:, FB : 2 * FB], val[:, 2 * FB : 3 * FB])
        for side in (0, 1):
            add(0, side, slice(0, FB), gd)
            add(0, side, slice(FB, 2 * FB), ud)
            add(1, side, slice(2 * FB, 3 * FB), hidden)

    for j in range(-(-2 * width // W)):

        @pl.when(k == groups + j)
        def _():
            for which, _, dst, cols in segments(j, width):
                for side in (0, 1):
                    add(which, side, slice(dst, dst + cols), val[:, dst : dst + cols])


def use(info, groups, width, val, own, sib, acc):
    count, rows = own.shape[0], own.shape[1]

    def chunk(i, info):
        return (jnp.clip(info[0], 0, count - 1), 0, 0)

    def kind(i, info):
        return (jnp.where(info[0] < groups, 0, 1), 0, 0, 0)

    tile = pl.BlockSpec((1,) + acc.shape[1:], kind)
    return pl.pallas_call(
        functools.partial(use_body, groups, width),
        grid_spec=pltpu.PrefetchScalarGridSpec(
            num_scalar_prefetch=1,
            grid=(1,),
            in_specs=[
                pl.BlockSpec(val.shape, lambda i, info: (0, 0)),
                pl.BlockSpec((1, rows, W), chunk),
                pl.BlockSpec((1, rows, W), chunk),
                tile,
            ],
            out_specs=tile,
        ),
        out_shape=jax.ShapeDtypeStruct(acc.shape, acc.dtype),
        input_output_aliases={4: 0},
        cost_estimate=pl.CostEstimate(
            flops=4 * rows * val.shape[0] * W,
            bytes_accessed=2 * (2 * rows + val.shape[0]) * W + 16 * rows * val.shape[0],
            transcendentals=val.shape[0] * FB,
        ),
        compiler_params=pltpu.CompilerParams(vmem_limit_bytes=VMEM),
    )(info, val, own, sib, acc)


def score_body(pieces, cand_hot, val_hot, *refs):
    out = refs[-1]
    kinds = (refs[:pieces], refs[pieces : 2 * pieces])
    for r in range(ROUNDS):
        sums = []
        for refs_of in kinds:
            for slot in (0, 1):
                total = refs_of[0][r, slot]
                for ref in refs_of[1:]:
                    total = total + ref[r, slot].astype(jnp.float32)
                sums.append(total)
        pair = sums[2] * sums[0] + sums[1] * sums[3]
        summed = jnp.dot(
            cand_hot[...],
            pair,
            precision=lax.Precision.HIGHEST,
            preferred_element_type=jnp.float32,
        )
        out[r] = jnp.dot(
            summed,
            val_hot[r],
            precision=lax.Precision.HIGHEST,
            preferred_element_type=jnp.float32,
        )


def score(cand_hot, val_hot, hidden_parts, input_parts):
    pieces = len(hidden_parts)
    return pl.pallas_call(
        functools.partial(score_body, pieces),
        out_shape=jax.ShapeDtypeStruct(
            (ROUNDS, cand_hot.shape[0], val_hot.shape[2]), jnp.float32
        ),
        compiler_params=pltpu.CompilerParams(vmem_limit_bytes=VMEM),
    )(cand_hot, val_hot, *hidden_parts, *input_parts)


def local(
    n_dp,
    n_tensor,
    cand_gate,
    cand_up,
    cand_dh,
    cand_x,
    cand_dy,
    val_gate,
    val_up,
    val_dh,
    val_x,
    val_dy,
    cand_lengths,
    val_lengths,
    round_owner,
):
    chips = n_dp // 2
    ring = list(range(chips // 2)) + list(range(chips - 1, chips // 2 - 1, -1))
    place = [ring.index(chip) for chip in range(chips)]
    along = []
    for i, chip in enumerate(ring):
        along.append((2 * chip, 2 * ring[(i + 1) % chips]))
        along.append((2 * chip + 1, 2 * ring[(i - 1) % chips] + 1))
    across = [(i, i ^ 1) for i in range(n_dp)]

    me = lax.axis_index("dp")
    at_z = lax.axis_index("tensor")
    core = me % 2
    places = jnp.asarray(place, jnp.int32)
    my_place = places[me // 2]

    cand_rows, val_rows = cand_x.shape[0], val_x.shape[0]
    half = val_rows // 2
    groups, width = cand_gate.shape[1] // FB, cand_x.shape[1]
    count = groups + -(-2 * width // W)
    vals = (val_gate, val_up, val_dh, val_x, val_dy)

    away, core_of = [], []
    for r in range(ROUNDS):
        owner = round_owner[r]
        behind = my_place - places[owner // 2]
        away.append(jnp.where(core == 0, behind, -behind) % chips)
        core_of.append((owner % 2 == core).astype(jnp.int32))

    cuts = [0, 1, 4, count]
    sib_parts = []
    for lo, hi in zip(cuts[:-1], cuts[1:]):
        part = pack((1 - core)[None], half, lo, hi - lo, False, *vals)
        sib_parts.append(lax.ppermute(part, "dp", across))

    def sib_of(t):
        for i, (lo, hi) in enumerate(zip(cuts[:-1], cuts[1:])):
            if lo <= t < hi:
                return sib_parts[i], t - lo

    cand_own = pack(
        jnp.zeros((1,), jnp.int32), cand_rows, 0, count, True,
        cand_gate, cand_up, cand_dh, cand_x, cand_dy,
    )
    cand_sib = lax.ppermute(cand_own, "dp", across)
    sib_lengths = lax.ppermute(cand_lengths, "dp", across)

    grams = [jnp.zeros((2, 2, 2 * cand_rows, half), jnp.float32) for _ in range(ROUNDS)]
    steps = count + chips - 1
    held = [[None] * steps for _ in range(ROUNDS)]
    got = [None] * ROUNDS
    used = 0
    parts = []

    def consume(t):
        for r in range(ROUNDS):
            k = (t - away[r])[None]
            grams[r] = use(k, groups, width, held[r][t], cand_own, cand_sib, grams[r])
        if t == groups + chips - 2:
            parts.append(scatter(0))

    block = 2 * cand_rows // n_tensor

    def scatter(kind):
        stacked = jnp.stack([g[kind] for g in grams], axis=0)

        def rows_of(z):
            return lax.dynamic_slice_in_dim(stacked, z * block, block, 2)

        out = [rows_of(at_z)]
        for m in range(1, n_tensor):
            piece = rows_of((at_z + m) % n_tensor).astype(jnp.bfloat16)
            out.append(
                lax.ppermute(piece, "tensor", [(z, (z + m) % n_tensor) for z in range(n_tensor)])
            )
        return out

    for t in range(steps):
        for r in range(ROUNDS):
            if t < count:
                info = jnp.stack([away[r], core_of[r], core])
                part, at = sib_of(t)
                held[r][t] = inject(t, at, half, info, *vals, part, got[r])
            else:
                held[r][t] = got[r]
            if t < steps - 1:
                got[r] = lax.ppermute(held[r][t], "dp", along)
        allowed = 0 if t < LAG else 2
        while allowed > 0 and used <= t:
            consume(used)
            used += 1
            allowed -= 1
    while used < steps:
        consume(used)
        used += 1
    parts.append(scatter(1))

    samples = cand_lengths.shape[1]
    segs = jnp.concatenate(
        [
            segment_of(cand_lengths[0], cand_rows),
            segment_of(sib_lengths[0], cand_rows) + samples,
        ]
    )
    segs = lax.dynamic_slice_in_dim(segs, at_z * block, block, 0)
    cand_hot = (jnp.arange(2 * samples, dtype=jnp.int32)[:, None] == segs[None, :]).astype(
        jnp.float32
    )
    hots, weights = [], []
    for r in range(ROUNDS):
        lengths = lax.dynamic_index_in_dim(val_lengths, round_owner[r], 0, keepdims=False)
        seg = lax.dynamic_slice_in_dim(segment_of(lengths, val_rows), core * half, half, 0)
        hots.append((seg[:, None] == jnp.arange(128, dtype=jnp.int32)[None, :]).astype(jnp.float32))
        weights.append(
            1.0
            / math.sqrt(D * FF)
            / jnp.sqrt(
                cand_lengths[0].astype(jnp.float32)[:, None]
                * lengths.astype(jnp.float32)[None, :]
            )
        )
    partial = score(cand_hot, jnp.stack(hots, axis=0), *parts)

    total = partial[:, :samples]
    for m in range(n_tensor):
        turn = [(z, (z + m) % n_tensor) for z in range(n_tensor)]
        if m > 0:
            total = total + lax.ppermute(partial[:, :samples], "tensor", turn)
        both = [
            (i * n_tensor + z, (i ^ 1) * n_tensor + (z + m) % n_tensor)
            for i in range(n_dp)
            for z in range(n_tensor)
        ]
        total = total + lax.ppermute(partial[:, samples:], ("dp", "tensor"), both)
    return total[:, :, : val_lengths.shape[1]] * jnp.stack(weights, axis=0)


def solution(mesh):
    n_dp, n_tensor = mesh.shape["dp"], mesh.shape["tensor"]
    in_specs = (P("dp", "tensor"),) * 10 + (P("dp", None), P(), P())
    return jax.shard_map(
        functools.partial(local, n_dp, n_tensor),
        mesh=mesh,
        in_specs=in_specs,
        out_specs=P(None, "dp", None),
        check_vma=False,
    )
```

```python
import functools
import math

import jax
import jax.numpy as jnp
from jax import lax
from jax.experimental import pallas as pl
from jax.experimental.pallas import tpu as pltpu
from jax.sharding import PartitionSpec as P

D = 8192
FF = 28672
ROUNDS = 2
FB = 512
W = 3 * FB
VMEM = 60 * 1024 * 1024

START = 10
NT = (((1,), (1,)), ((), ()))


def derive(gate, up, grad_hidden):
    gate_f = gate.astype(jnp.float32)
    up_f = up.astype(jnp.float32)
    grad_f = grad_hidden.astype(jnp.float32)
    sigmoid_gate = jax.nn.sigmoid(gate_f)
    activated = gate_f * sigmoid_gate
    hidden = (activated * up_f).astype(jnp.bfloat16)
    grad_gate = (grad_f * up_f * sigmoid_gate * (1.0 + gate_f * (1.0 - sigmoid_gate))).astype(
        jnp.bfloat16
    )
    grad_up = (grad_f * activated).astype(jnp.bfloat16)
    return (grad_gate, grad_up, hidden)


def segment_of(lengths, total):
    bounds = jnp.cumsum(lengths)
    position = jnp.arange(total, dtype=jnp.int32)
    return jnp.sum((position[:, None] >= bounds[None, :]).astype(jnp.int32), axis=1)


def segments(j, width):
    out = []
    for which in (0, 1):
        lo = max(j * W, which * width)
        hi = min((j + 1) * W, (which + 1) * width)
        if hi > lo:
            out.append((which, lo - which * width, lo - j * W, hi - lo))
    return out


def pack_body(groups, width, first, transform, half, gate, up, dh, x, dy, *rest):
    out = rest[-2]
    k = pl.program_id(0) + first

    @pl.when(k < groups)
    def _():
        if transform:
            a, b, c = derive(gate[...], up[...], dh[...])
        else:
            a, b, c = gate[...], up[...], dh[...]
        out[0, :, 0:FB] = a
        out[0, :, FB : 2 * FB] = b
        out[0, :, 2 * FB : 3 * FB] = c

    for j in range(-(-2 * width // W)):

        @pl.when(k == groups + j)
        def _():
            end = 0
            for which, src, dst, cols in segments(j, width):
                out[0, :, dst : dst + cols] = (x, dy)[which][:, src : src + cols]
                end = dst + cols
            if end < W:
                out[0, :, end:W] = jnp.zeros((out.shape[1], W - end), out.dtype)


ANYWHERE = pl.BlockSpec(memory_space=pl.ANY)
IN_HBM = pl.BlockSpec(memory_space=pltpu.HBM)
MARK = jax.ShapeDtypeStruct((8, 128), jnp.float32)


def pack(half, rows, base, first, count, size, transform, held, deps, *arrays):
    groups, width = arrays[0].shape[1] // FB, arrays[3].shape[1]
    shift = first - base
    extra = ([] if held is None else [held]) + list(deps)
    wide = pl.BlockSpec(
        (rows, FB), lambda k, half: (half[0], jnp.minimum(k + first, groups - 1))
    )
    flat = pl.BlockSpec((rows, width), lambda k, half: (half[0], 0))
    return pl.pallas_call(
        functools.partial(pack_body, groups, width, first, transform),
        grid_spec=pltpu.PrefetchScalarGridSpec(
            num_scalar_prefetch=1,
            grid=(count,),
            in_specs=[wide, wide, wide, flat, flat] + [ANYWHERE] * len(extra),
            out_specs=[pl.BlockSpec((1, rows, W), lambda k, half: (k + shift, 0, 0)), IN_HBM],
        ),
        out_shape=[jax.ShapeDtypeStruct((size, rows, W), jnp.bfloat16), MARK],
        input_output_aliases={} if held is None else {6: 0},
        cost_estimate=pl.CostEstimate(
            flops=20 * count * rows * W if transform else 0,
            bytes_accessed=4 * count * rows * W,
            transcendentals=count * rows * FB if transform else 0,
        ),
        compiler_params=pltpu.CompilerParams(vmem_limit_bytes=VMEM),
    )(half, *arrays, *extra)


def inject_body(t, at, groups, width, always, info, gate, up, dh, x, dy, sib, *rest):
    out, room, sem = rest[-3:]
    rows = out.shape[0]
    start = pl.multiple_of(info[2] * rows, rows)
    mine = info[1] == 1
    first = jnp.logical_or(always, info[0] == 0)

    if t < groups:
        parts = [
            (ref.at[pl.ds(start, rows), pl.ds(t * FB, FB)], room.at[:, pl.ds(i * FB, FB)])
            for i, ref in enumerate((gate, up, dh))
        ]
    else:
        parts = [
            (
                (x, dy)[which].at[pl.ds(start, rows), pl.ds(src, cols)],
                room.at[:, pl.ds(dst, cols)],
            )
            for which, src, dst, cols in segments(t - groups, width)
        ]

    @pl.when(first)
    def _():
        @pl.when(mine)
        def _():
            copies = [pltpu.make_async_copy(a, b, sem.at[i]) for i, (a, b) in enumerate(parts)]
            for copy in copies:
                copy.start()
            for copy in copies:
                copy.wait()

        @pl.when(jnp.logical_not(mine))
        def _():
            copy = pltpu.make_async_copy(sib.at[at], room, sem.at[0])
            copy.start()
            copy.wait()

        copy = pltpu.make_async_copy(room, out, sem.at[0])
        copy.start()
        copy.wait()


def inject(t, at, rows, info, vals, sib, held, deps):
    groups, width = vals[0].shape[1] // FB, vals[3].shape[1]
    extra = ([] if held is None else [held]) + list(deps)
    return pl.pallas_call(
        functools.partial(inject_body, t, at, groups, width, held is None),
        in_specs=[pl.BlockSpec(memory_space=pltpu.SMEM)]
        + [IN_HBM] * (6 if held is None else 7)
        + [ANYWHERE] * len(deps),
        out_specs=IN_HBM,
        out_shape=jax.ShapeDtypeStruct((rows, W), jnp.bfloat16),
        scratch_shapes=[pltpu.VMEM((rows, W), jnp.bfloat16), pltpu.SemaphoreType.DMA((3,))],
        input_output_aliases={} if held is None else {7: 0},
        cost_estimate=pl.CostEstimate(
            flops=0, bytes_accessed=4 * rows * W, transcendentals=0
        ),
        compiler_params=pltpu.CompilerParams(vmem_limit_bytes=VMEM),
    )(info, *vals, sib, *extra)


def use_body(t, groups, width, bounds, info, *refs):
    r = pl.program_id(0)
    vals, pieces = refs[:ROUNDS], refs[ROUNDS : ROUNDS + 2 * len(bounds)]
    acc_in, acc = refs[ROUNDS + 2 * len(bounds)], refs[-2]
    k = t - info[r]
    acc[...] = acc_in[...]
    rows = pieces[0].shape[1]

    def add(slot, pair, cols, right):
        for side in (0, 1):
            left = pair[side][0, :, cols]
            acc[0, 0, slot, side * rows : (side + 1) * rows, :] += lax.dot_general(
                left, right, NT, preferred_element_type=jnp.float32
            )

    for i, (lo, hi) in enumerate(bounds):
        pair = pieces[2 * i : 2 * i + 2]
        for q in range(ROUNDS):
            val = vals[q]

            @pl.when((r == q) & (k >= lo) & (k < min(hi, groups)))
            def _():
                gd, ud, hidden = derive(val[:, 0:FB], val[:, FB : 2 * FB], val[:, 2 * FB : 3 * FB])
                add(0, pair, slice(0, FB), gd)
                add(0, pair, slice(FB, 2 * FB), ud)
                add(1, pair, slice(2 * FB, 3 * FB), hidden)

            for j in range(-(-2 * width // W)):
                if lo <= groups + j < hi:

                    @pl.when((r == q) & (k == groups + j))
                    def _():
                        for which, _, dst, cols in segments(j, width):
                            add(which, pair, slice(dst, dst + cols), val[:, dst : dst + cols])


def use(t, info, groups, width, vals, bounds, pieces, acc, deps):
    rows = pieces[0].shape[1]
    in_specs = [pl.BlockSpec(vals[0].shape, lambda r, info: (0, 0))] * ROUNDS
    for lo, hi in bounds:

        def chunk(r, info, lo=lo, hi=hi):
            return (jnp.clip(t - info[r], lo, hi - 1) - lo, 0, 0)

        in_specs += [pl.BlockSpec((1, rows, W), chunk)] * 2

    def kind(r, info):
        return (r, jnp.where(t - info[r] < groups, 0, 1), 0, 0, 0)

    tile = pl.BlockSpec((1, 1) + acc.shape[2:], kind)
    return pl.pallas_call(
        functools.partial(use_body, t, groups, width, bounds),
        grid_spec=pltpu.PrefetchScalarGridSpec(
            num_scalar_prefetch=1,
            grid=(ROUNDS,),
            in_specs=in_specs + [tile] + [ANYWHERE] * len(deps),
            out_specs=[tile, IN_HBM],
        ),
        out_shape=[jax.ShapeDtypeStruct(acc.shape, acc.dtype), MARK],
        input_output_aliases={len(in_specs) + 1: 0},
        cost_estimate=pl.CostEstimate(
            flops=8 * rows * vals[0].shape[0] * W,
            bytes_accessed=4 * (2 * rows + vals[0].shape[0]) * W,
            transcendentals=ROUNDS * vals[0].shape[0] * FB,
        ),
        compiler_params=pltpu.CompilerParams(vmem_limit_bytes=VMEM),
    )(info, *vals, *pieces, acc, *deps)


def cut_body(pieces, at, acc, own, *others):
    block = own.shape[2]
    for m in range(pieces):
        rows = pl.ds(pl.multiple_of(lax.rem(at[0] + m, pieces) * block, block), block)
        for r in range(ROUNDS):
            for slot in (0, 1):
                tile = acc[r, 0, slot, rows, :]
                if m == 0:
                    own[r, slot] = tile
                else:
                    others[m - 1][r, slot] = tile.astype(jnp.bfloat16)


def cut(kind, at_z, pieces, acc):
    block, half = acc.shape[3] // pieces, acc.shape[4]
    shape = (ROUNDS, 2, block, half)
    whole = pl.BlockSpec(shape, lambda i, at: (0, 0, 0, 0))
    return pl.pallas_call(
        functools.partial(cut_body, pieces),
        grid_spec=pltpu.PrefetchScalarGridSpec(
            num_scalar_prefetch=1,
            grid=(1,),
            in_specs=[
                pl.BlockSpec((ROUNDS, 1) + acc.shape[2:], lambda i, at: (0, kind, 0, 0, 0))
            ],
            out_specs=[whole] * pieces,
        ),
        out_shape=[jax.ShapeDtypeStruct(shape, jnp.float32)]
        + [jax.ShapeDtypeStruct(shape, jnp.bfloat16)] * (pieces - 1),
        cost_estimate=pl.CostEstimate(flops=0, bytes_accessed=8 * acc.size, transcendentals=0),
        compiler_params=pltpu.CompilerParams(vmem_limit_bytes=VMEM),
    )(at_z[None], acc)


def score_body(pieces, cand_hot, val_hot, *refs):
    out = refs[-1]
    kinds = (refs[:pieces], refs[pieces : 2 * pieces])
    for r in range(ROUNDS):
        sums = []
        for refs_of in kinds:
            for slot in (0, 1):
                total = refs_of[0][r, slot]
                for ref in refs_of[1:]:
                    total = total + ref[r, slot].astype(jnp.float32)
                sums.append(total)
        pair = sums[2] * sums[0] + sums[1] * sums[3]
        summed = jnp.dot(
            cand_hot[...],
            pair,
            precision=lax.Precision.HIGHEST,
            preferred_element_type=jnp.float32,
        )
        out[r] = jnp.dot(
            summed,
            val_hot[r],
            precision=lax.Precision.HIGHEST,
            preferred_element_type=jnp.float32,
        )


def score(cand_hot, val_hot, hidden_parts, input_parts):
    pieces = len(hidden_parts)
    return pl.pallas_call(
        functools.partial(score_body, pieces),
        out_shape=jax.ShapeDtypeStruct(
            (ROUNDS, cand_hot.shape[0], val_hot.shape[2]), jnp.float32
        ),
        compiler_params=pltpu.CompilerParams(vmem_limit_bytes=VMEM),
    )(cand_hot, val_hot, *hidden_parts, *input_parts)


def local(
    n_dp,
    n_tensor,
    cand_gate,
    cand_up,
    cand_dh,
    cand_x,
    cand_dy,
    val_gate,
    val_up,
    val_dh,
    val_x,
    val_dy,
    cand_lengths,
    val_lengths,
    round_owner,
):
    chips = n_dp // 2
    ring = list(range(chips // 2)) + list(range(chips - 1, chips // 2 - 1, -1))
    place = [ring.index(chip) for chip in range(chips)]
    along = []
    for i, chip in enumerate(ring):
        along.append((2 * chip, 2 * ring[(i + 1) % chips]))
        along.append((2 * chip + 1, 2 * ring[(i - 1) % chips] + 1))
    across = [(i, i ^ 1) for i in range(n_dp)]

    me = lax.axis_index("dp")
    at_z = lax.axis_index("tensor")
    core = me % 2
    places = jnp.asarray(place, jnp.int32)
    my_place = places[me // 2]

    cand_rows, val_rows = cand_x.shape[0], val_x.shape[0]
    half = val_rows // 2
    groups, width = cand_gate.shape[1] // FB, cand_x.shape[1]
    count = groups + -(-2 * width // W)
    vals = (val_gate, val_up, val_dh, val_x, val_dy)

    away, core_of = [], []
    for r in range(ROUNDS):
        owner = round_owner[r]
        behind = my_place - places[owner // 2]
        away.append(jnp.where(core == 0, behind, -behind) % chips)
        core_of.append((owner % 2 == core).astype(jnp.int32))

    sib_lengths = lax.ppermute(cand_lengths, "dp", across)

    info = [jnp.stack([away[r], core_of[r], core]) for r in range(ROUNDS)]
    aways = jnp.stack(away)
    other = (1 - core)[None]
    both = jnp.zeros((1,), jnp.int32)

    sib_parts = [None] * count

    def send_half(lo, hi, deps):
        part, mark = pack(other, half, lo, lo, hi - lo, hi - lo, False, None, deps, *vals)
        part = lax.ppermute(part, "dp", across)
        for t in range(lo, hi):
            sib_parts[t] = (part, t - lo)
        return mark

    middle = min(groups, max(1, count // 2))
    bounds = [(0, middle), (middle, count)]
    cand_own, cand_sib = [None, None], [None, None]

    def derive_some(i, lo, hi, deps):
        base, end = bounds[i]
        cand_own[i], mark = pack(
            both, cand_rows, base, lo, hi - lo, end - base, True, cand_own[i], deps,
            cand_gate, cand_up, cand_dh, cand_x, cand_dy,
        )
        if hi == end:
            cand_sib[i] = lax.ppermute(cand_own[i], "dp", across)
        return mark

    grams = [jnp.zeros((ROUNDS, 2, 2, 2 * cand_rows, half), jnp.float32)]
    steps = count + chips - 1
    held = [[None] * steps for _ in range(ROUNDS)]
    got = [None] * ROUNDS
    parts, wait_for = [], []

    def scatter(kind):
        pieces = cut(kind, at_z, n_tensor, grams[0])
        wait_for[:] = [pieces[0]]
        return [pieces[0]] + [
            lax.ppermute(pieces[m], "tensor", [(z, (z + m) % n_tensor) for z in range(n_tensor)])
            for m in range(1, n_tensor)
        ]

    def consume(t, deps):
        low, high = t - (chips - 1), t
        needed = [i for i, (lo, hi) in enumerate(bounds) if low < hi and high >= lo]
        pieces = []
        for i in needed:
            pieces += [cand_own[i], cand_sib[i]]
        grams[0], mark = use(
            t, aways, groups, width, [held[r][t] for r in range(ROUNDS)],
            [bounds[i] for i in needed], pieces, grams[0], deps + wait_for,
        )
        wait_for[:] = []
        if t == groups + chips - 2:
            parts.append(scatter(0))
        return mark

    work = []
    cuts = [c for c in (4, 8, 12) if c < count] + [count]
    for lo, hi in zip(cuts[:-1], cuts[1:]):
        work.append((0, functools.partial(send_half, lo, hi)))
    for i, (lo, hi) in enumerate(bounds):
        for a in range(lo, hi, 3):
            work.append((0, functools.partial(derive_some, i, a, min(a + 3, hi))))
    for t in range(steps):
        work.append((max(t * ROUNDS + ROUNDS - 1, START), functools.partial(consume, t)))

    mark = send_half(0, 1, [])
    mark = send_half(1, min(4, count), [mark])
    slot = 0
    for t in range(steps):
        for r in range(ROUNDS):
            if t < count:
                part, at = sib_parts[t]
                held[r][t] = inject(t, at, half, info[r], vals, part, got[r], [mark])
            else:
                held[r][t] = got[r]
            if t < steps - 1:
                got[r] = lax.ppermute(held[r][t], "dp", along)
            if work and work[0][0] <= slot:
                mark = work.pop(0)[1]([held[r][t]])
            slot += 1
    while work:
        mark = work.pop(0)[1]([mark])
    parts.append(scatter(1))
    block = 2 * cand_rows // n_tensor

    samples = cand_lengths.shape[1]
    segs = jnp.concatenate(
        [
            segment_of(cand_lengths[0], cand_rows),
            segment_of(sib_lengths[0], cand_rows) + samples,
        ]
    )
    segs = lax.dynamic_slice_in_dim(segs, at_z * block, block, 0)
    cand_hot = (jnp.arange(2 * samples, dtype=jnp.int32)[:, None] == segs[None, :]).astype(
        jnp.float32
    )
    hots, weights = [], []
    for r in range(ROUNDS):
        lengths = lax.dynamic_index_in_dim(val_lengths, round_owner[r], 0, keepdims=False)
        seg = lax.dynamic_slice_in_dim(segment_of(lengths, val_rows), core * half, half, 0)
        hots.append((seg[:, None] == jnp.arange(128, dtype=jnp.int32)[None, :]).astype(jnp.float32))
        weights.append(
            1.0
            / math.sqrt(D * FF)
            / jnp.sqrt(
                cand_lengths[0].astype(jnp.float32)[:, None]
                * lengths.astype(jnp.float32)[None, :]
            )
        )
    partial = score(cand_hot, jnp.stack(hots, axis=0), *parts)

    total = partial[:, :samples]
    for m in range(n_tensor):
        turn = [(z, (z + m) % n_tensor) for z in range(n_tensor)]
        if m > 0:
            total = total + lax.ppermute(partial[:, :samples], "tensor", turn)
        both = [
            (i * n_tensor + z, (i ^ 1) * n_tensor + (z + m) % n_tensor)
            for i in range(n_dp)
            for z in range(n_tensor)
        ]
        total = total + lax.ppermute(partial[:, samples:], ("dp", "tensor"), both)
    return total[:, :, : val_lengths.shape[1]] * jnp.stack(weights, axis=0)


def solution(mesh):
    n_dp, n_tensor = mesh.shape["dp"], mesh.shape["tensor"]
    in_specs = (P("dp", "tensor"),) * 10 + (P("dp", None), P(), P())
    return jax.shard_map(
        functools.partial(local, n_dp, n_tensor),
        mesh=mesh,
        in_specs=in_specs,
        out_specs=P(None, "dp", None),
        check_vma=False,
    )
```

```python
import functools
import math

import jax
import jax.numpy as jnp
from jax import lax
from jax.experimental import pallas as pl
from jax.experimental.pallas import tpu as pltpu
from jax.sharding import PartitionSpec as P

D = 8192
FF = 28672
ROUNDS = 2
FB = 512
W = 3 * FB
VMEM = 64 * 1024 * 1024 - 256 * 1024

START = 11
NT = (((1,), (1,)), ((), ()))


def derive(gate, up, grad_hidden):
    gate_f = gate.astype(jnp.float32)
    up_f = up.astype(jnp.float32)
    grad_f = grad_hidden.astype(jnp.float32)
    sigmoid_gate = jax.nn.sigmoid(gate_f)
    activated = gate_f * sigmoid_gate
    hidden = (activated * up_f).astype(jnp.bfloat16)
    grad_gate = (grad_f * up_f * sigmoid_gate * (1.0 + gate_f * (1.0 - sigmoid_gate))).astype(
        jnp.bfloat16
    )
    grad_up = (grad_f * activated).astype(jnp.bfloat16)
    return (grad_gate, grad_up, hidden)


def segment_of(lengths, total):
    bounds = jnp.cumsum(lengths)
    position = jnp.arange(total, dtype=jnp.int32)
    return jnp.sum((position[:, None] >= bounds[None, :]).astype(jnp.int32), axis=1)


def segments(j, width):
    out = []
    for which in (0, 1):
        lo = max(j * W, which * width)
        hi = min((j + 1) * W, (which + 1) * width)
        if hi > lo:
            out.append((which, lo - which * width, lo - j * W, hi - lo))
    return out


ANYWHERE = pl.BlockSpec(memory_space=pl.ANY)
IN_HBM = pl.BlockSpec(memory_space=pltpu.HBM)
IN_SMEM = pl.BlockSpec(memory_space=pltpu.SMEM)
MARK = jax.ShapeDtypeStruct((8, 128), jnp.float32)


def place_of(chip, chips):
    return jnp.where(chip < chips // 2, chip, chips // 2 + chips - 1 - chip)


def away_of(me, owner, chips):
    behind = place_of(me // 2, chips) - place_of(owner // 2, chips)
    return lax.rem(jnp.where(me % 2 == 0, behind, -behind) + chips, chips)


def pack_body(groups, width, first, half, gate, up, dh, x, dy, *rest):
    out = rest[-2]
    k = pl.program_id(0) + first

    @pl.when(k < groups)
    def _():
        out[0, :, 0:FB] = gate[...]
        out[0, :, FB : 2 * FB] = up[...]
        out[0, :, 2 * FB : 3 * FB] = dh[...]

    for j in range(-(-2 * width // W)):

        @pl.when(k == groups + j)
        def _():
            end = 0
            for which, src, dst, cols in segments(j, width):
                out[0, :, dst : dst + cols] = (x, dy)[which][:, src : src + cols]
                end = dst + cols
            if end < W:
                out[0, :, end:W] = jnp.zeros((out.shape[1], W - end), out.dtype)


def pack(half, rows, first, count, deps, *arrays):
    groups, width = arrays[0].shape[1] // FB, arrays[3].shape[1]
    wide = pl.BlockSpec(
        (rows, FB), lambda k, half: (half[0], jnp.minimum(k + first, groups - 1))
    )
    flat = pl.BlockSpec((rows, width), lambda k, half: (half[0], 0))
    return pl.pallas_call(
        functools.partial(pack_body, groups, width, first),
        grid_spec=pltpu.PrefetchScalarGridSpec(
            num_scalar_prefetch=1,
            grid=(count,),
            in_specs=[wide, wide, wide, flat, flat] + [ANYWHERE] * len(deps),
            out_specs=[pl.BlockSpec((1, rows, W), lambda k, half: (k, 0, 0)), IN_HBM],
        ),
        out_shape=[jax.ShapeDtypeStruct((count, rows, W), jnp.bfloat16), MARK],
        cost_estimate=pl.CostEstimate(
            flops=0, bytes_accessed=4 * count * rows * W, transcendentals=0
        ),
        compiler_params=pltpu.CompilerParams(vmem_limit_bytes=VMEM),
    )(half, *arrays, *deps)


def inject_body(t, at, r, groups, width, n_dp, always, owner, gate, up, dh, x, dy, sib, *rest):
    out, room, sem = rest[-3:]
    rows = out.shape[0]
    me = lax.axis_index("dp")
    start = pl.multiple_of(me % 2 * rows, rows)
    mine = owner[r] % 2 == me % 2
    first = jnp.logical_or(always, owner[r] // 2 == me // 2)

    if t < groups:
        parts = [(ref, t * FB, i * FB, FB) for i, ref in enumerate((gate, up, dh))]
    else:
        parts = [
            ((x, dy)[which], src, dst, cols)
            for which, src, dst, cols in segments(t - groups, width)
        ]

    def through(sources):
        ins, outs = [], []
        for i, (source, dst, cols) in enumerate(sources):
            ins.append(pltpu.make_async_copy(source, room.at[:, pl.ds(dst, cols)], sem.at[0, i]))
            outs.append(
                pltpu.make_async_copy(
                    room.at[:, pl.ds(dst, cols)], out.at[:, pl.ds(dst, cols)], sem.at[1, i]
                )
            )
        for copy in ins:
            copy.start()
        for before, copy in zip(ins, outs):
            before.wait()
            copy.start()
        for copy in outs:
            copy.wait()

    @pl.when(first)
    def _():
        @pl.when(mine)
        def _():
            through(
                [(ref.at[pl.ds(start, rows), pl.ds(src, cols)], dst, cols) for ref, src, dst, cols in parts]
            )

        @pl.when(jnp.logical_not(mine))
        def _():
            through([(sib.at[at, :, pl.ds(i * FB, FB)], i * FB, FB) for i in range(3)])


def inject(t, at, r, rows, n_dp, owner, vals, sib, held, deps):
    groups, width = vals[0].shape[1] // FB, vals[3].shape[1]
    extra = ([] if held is None else [held]) + list(deps)
    return pl.pallas_call(
        functools.partial(inject_body, t, at, r, groups, width, n_dp, held is None),
        in_specs=[IN_SMEM]
        + [IN_HBM] * (6 if held is None else 7)
        + [ANYWHERE] * len(deps),
        out_specs=IN_HBM,
        out_shape=jax.ShapeDtypeStruct((rows, W), jnp.bfloat16),
        scratch_shapes=[pltpu.VMEM((rows, W), jnp.bfloat16), pltpu.SemaphoreType.DMA((2, 3))],
        input_output_aliases={} if held is None else {7: 0},
        cost_estimate=pl.CostEstimate(
            flops=0, bytes_accessed=4 * rows * W, transcendentals=0
        ),
        compiler_params=pltpu.CompilerParams(vmem_limit_bytes=VMEM),
    )(owner, *vals, sib, *extra)


def use_body(k, groups, width, chips, fresh, owner, own, sib, held, accs_in, accs, room, val, sums, sem):
    rows = room.shape[1]
    half = val.shape[0] // ROUNDS
    me = lax.axis_index("dp")
    brought = []
    for r in range(ROUNDS):
        away = away_of(me, owner[r], chips)
        there = val.at[pl.ds(r * half, half)]
        for i in range(chips):

            @pl.when(away == i)
            def _():
                pltpu.make_async_copy(held[r * chips + i], there, sem.at[r]).start()

        brought.append(pltpu.make_async_copy(held[r * chips], there, sem.at[r]))
    if k < groups:
        parts = [(i, k * FB, i * FB, FB) for i in range(3)]
    else:
        parts = [(3 + which, src, dst, cols) for which, src, dst, cols in segments(k - groups, width)]
    loads = []
    for side, arrays in enumerate((own, sib)):
        loads.append([])
        for i, (which, src, dst, cols) in enumerate(parts):
            copy = pltpu.make_async_copy(
                arrays[which].at[:, pl.ds(src, cols)],
                room.at[side, :, pl.ds(dst, cols)],
                sem.at[2 + 3 * side + i],
            )
            copy.start()
            loads[side].append(copy)
    priors, slot = [], 0
    slots = []
    for i, acc in enumerate(accs):
        n = acc.shape[0]
        slots.append((slot, n))
        if not fresh[i]:
            copy = pltpu.make_async_copy(accs_in.pop(0), sums.at[pl.ds(slot, n)], sem.at[8 + i])
            copy.start()
            priors.append(copy)
        slot += n

    for copy in brought:
        copy.wait()
    if k < groups:
        rights = derive(val[:, 0:FB], val[:, FB : 2 * FB], val[:, 2 * FB : 3 * FB])
    for copy in priors:
        copy.wait()
    stores = []
    for side in (0, 1):
        for copy in loads[side]:
            copy.wait()
        at = pl.ds(side * rows, rows)

        def dot(left, right):
            return lax.dot_general(left, right, NT, preferred_element_type=jnp.float32)

        if k < groups:
            lefts = derive(*(room[side, :, i * FB : (i + 1) * FB] for i in range(3)))
            terms = [
                dot(lefts[0], rights[0]) + dot(lefts[1], rights[1]),
                dot(lefts[2], rights[2]),
            ]
        else:
            terms = [
                dot(room[side, :, dst : dst + cols], val[:, dst : dst + cols])
                for _, _, dst, cols in parts
            ]
        for i, term in enumerate(terms):
            if fresh[i if len(accs) > 1 else 0]:
                sums[i, at, :] = term
            else:
                sums[i, at, :] += term
        for i, acc in enumerate(accs):
            first, n = slots[i]
            copy = pltpu.make_async_copy(
                sums.at[pl.ds(first, n), at], acc.at[:, at], sem.at[10 + 2 * side + i]
            )
            copy.start()
            stores.append(copy)
    for copy in stores:
        copy.wait()


def use(k, owner, groups, width, chips, own, sib, held, grams, deps):
    cand_rows, half = own[0].shape[0], held[0].shape[0]
    if k < groups:
        names = [("gu_h", 2)]
    else:
        names = [(("x", "dy")[which], 1) for which, _, _, _ in segments(k - groups, width)]
    fresh = [name not in grams for name, _ in names]
    priors = [grams[name] for name, _ in names if name in grams]
    shapes = [
        jax.ShapeDtypeStruct((n, 2 * cand_rows, ROUNDS * half), jnp.float32) for _, n in names
    ]
    n_cand, n_held = len(own), len(held)

    def body(owner, *refs):
        a, b = n_cand, 2 * n_cand
        c = b + n_held
        d = c + len(priors)
        e = d + len(deps)
        f = e + len(shapes)
        use_body(
            k, groups, width, chips, fresh, owner, refs[:a], refs[a:b], refs[b:c],
            list(refs[c:d]), refs[e:f], *refs[f + 1 :],
        )

    results = pl.pallas_call(
        body,
        in_specs=[IN_SMEM]
        + [IN_HBM] * (2 * n_cand + n_held + len(priors))
        + [ANYWHERE] * len(deps),
        out_specs=[IN_HBM] * (len(shapes) + 1),
        out_shape=shapes + [MARK],
        scratch_shapes=[
            pltpu.VMEM((2, cand_rows, W), jnp.bfloat16),
            pltpu.VMEM((ROUNDS * half, W), jnp.bfloat16),
            pltpu.VMEM((2, 2 * cand_rows, ROUNDS * half), jnp.float32),
            pltpu.SemaphoreType.DMA((14,)),
        ],
        cost_estimate=pl.CostEstimate(
            flops=8 * cand_rows * half * W,
            bytes_accessed=4 * (cand_rows + half) * W + 32 * cand_rows * half,
            transcendentals=2 * (cand_rows + half) * FB,
        ),
        compiler_params=pltpu.CompilerParams(vmem_limit_bytes=VMEM),
    )(owner, *own, *sib, *held, *priors, *deps)
    for (name, _), value in zip(names, results):
        grams[name] = value
    return results[-1]


def cut_body(pieces, at, acc, own, *others):
    block = own.shape[1]
    for m in range(pieces):
        rows = pl.ds(pl.multiple_of(lax.rem(at[0] + m, pieces) * block, block), block)
        tile = acc[:, rows, :]
        if m == 0:
            own[...] = tile
        else:
            others[m - 1][...] = tile.astype(jnp.bfloat16)


def cut(at_z, pieces, acc):
    shape = (acc.shape[0], acc.shape[1] // pieces, acc.shape[2])
    whole = pl.BlockSpec(shape, lambda i, at: (0, 0, 0))
    return pl.pallas_call(
        functools.partial(cut_body, pieces),
        grid_spec=pltpu.PrefetchScalarGridSpec(
            num_scalar_prefetch=1,
            grid=(1,),
            in_specs=[pl.BlockSpec(acc.shape, lambda i, at: (0, 0, 0))],
            out_specs=[whole] * pieces,
        ),
        out_shape=[jax.ShapeDtypeStruct(shape, jnp.float32)]
        + [jax.ShapeDtypeStruct(shape, jnp.bfloat16)] * (pieces - 1),
        cost_estimate=pl.CostEstimate(flops=0, bytes_accessed=8 * acc.size, transcendentals=0),
        compiler_params=pltpu.CompilerParams(vmem_limit_bytes=VMEM),
    )(at_z[None], acc)


def score_body(pieces, cand_hot, val_hot, *refs):
    out = refs[-1]

    def total(i, slot):
        value = refs[i * pieces][slot]
        for ref in refs[i * pieces + 1 : (i + 1) * pieces]:
            value = value + ref[slot].astype(jnp.float32)
        return value

    pair = total(1, 0) * total(0, 0) + total(0, 1) * total(2, 0)
    half = pair.shape[1] // ROUNDS
    summed = jnp.dot(
        cand_hot[...],
        pair,
        precision=lax.Precision.HIGHEST,
        preferred_element_type=jnp.float32,
    )
    for r in range(ROUNDS):
        out[r] = jnp.dot(
            summed[:, r * half : (r + 1) * half],
            val_hot[r],
            precision=lax.Precision.HIGHEST,
            preferred_element_type=jnp.float32,
        )


def score(cand_hot, val_hot, gu_h, x, dy):
    return pl.pallas_call(
        functools.partial(score_body, len(x)),
        out_shape=jax.ShapeDtypeStruct(
            (ROUNDS, cand_hot.shape[0], val_hot.shape[2]), jnp.float32
        ),
        compiler_params=pltpu.CompilerParams(vmem_limit_bytes=VMEM),
    )(cand_hot, val_hot, *gu_h, *x, *dy)


def local(
    n_dp,
    n_tensor,
    cand_gate,
    cand_up,
    cand_dh,
    cand_x,
    cand_dy,
    val_gate,
    val_up,
    val_dh,
    val_x,
    val_dy,
    cand_lengths,
    val_lengths,
    round_owner,
):
    chips = n_dp // 2
    ring = list(range(chips // 2)) + list(range(chips - 1, chips // 2 - 1, -1))
    along = []
    for i, chip in enumerate(ring):
        along.append((2 * chip, 2 * ring[(i + 1) % chips]))
        along.append((2 * chip + 1, 2 * ring[(i - 1) % chips] + 1))
    across = [(i, i ^ 1) for i in range(n_dp)]

    at_z = lax.axis_index("tensor")
    core = lax.axis_index("dp") % 2

    cand_rows, val_rows = cand_x.shape[0], val_x.shape[0]
    half = val_rows // 2
    groups, width = cand_gate.shape[1] // FB, cand_x.shape[1]
    count = groups + -(-2 * width // W)
    vals = (val_gate, val_up, val_dh, val_x, val_dy)
    own = (cand_gate, cand_up, cand_dh, cand_x, cand_dy)
    other = (1 - core)[None]

    sib_parts = [None] * count

    def send_half(lo, hi, deps):
        part, mark = pack(other, half, lo, hi - lo, deps, *vals)
        part = lax.ppermute(part, "dp", across)
        for t in range(lo, hi):
            sib_parts[t] = (part, t - lo)
        return mark

    mark = send_half(0, 1, [])
    mark = send_half(1, min(4, count), [mark])
    sib = [lax.ppermute(array, "dp", across) for array in own]
    sib_lengths = lax.ppermute(cand_lengths, "dp", across)

    grams, parts = {}, {}
    steps = count + chips - 1
    held = [[None] * steps for _ in range(ROUNDS)]
    got = [None] * ROUNDS

    def scatter(name):
        pieces = cut(at_z, n_tensor, grams[name])
        parts[name] = [pieces[0]] + [
            lax.ppermute(pieces[m], "tensor", [(z, (z + m) % n_tensor) for z in range(n_tensor)])
            for m in range(1, n_tensor)
        ]

    last_of = {"gu_h": groups - 1}
    for k in range(groups, count):
        for which, _, _, _ in segments(k - groups, width):
            last_of[("x", "dy")[which]] = k

    def consume(k, deps):
        came = [held[r][k + i] for r in range(ROUNDS) for i in range(chips)]
        mark = use(k, round_owner, groups, width, chips, own, sib, came, grams, deps)
        for name in last_of:
            if last_of[name] == k:
                scatter(name)
        return mark

    work = []
    cuts = [c for c in (4, 8, 12) if c < count] + [count]
    for lo, hi in zip(cuts[:-1], cuts[1:]):
        work.append((0, functools.partial(send_half, lo, hi)))
    for k in range(count):
        work.append((max((k + chips) * ROUNDS - 1, START), functools.partial(consume, k)))

    slot = 0
    for t in range(steps):
        for r in range(ROUNDS):
            if t < count:
                part, at = sib_parts[t]
                held[r][t] = inject(t, at, r, half, n_dp, round_owner, vals, part, got[r], [mark])
            else:
                held[r][t] = got[r]
            if t < steps - 1:
                got[r] = lax.ppermute(held[r][t], "dp", along)
            if work and work[0][0] <= slot:
                mark = work.pop(0)[1]([held[r][t]])
            slot += 1
    while work:
        mark = work.pop(0)[1]([mark])

    block = 2 * cand_rows // n_tensor
    samples = cand_lengths.shape[1]
    segs = jnp.concatenate(
        [
            segment_of(cand_lengths[0], cand_rows),
            segment_of(sib_lengths[0], cand_rows) + samples,
        ]
    )
    segs = lax.dynamic_slice_in_dim(segs, at_z * block, block, 0)
    cand_hot = (jnp.arange(2 * samples, dtype=jnp.int32)[:, None] == segs[None, :]).astype(
        jnp.float32
    )
    hots, weights = [], []
    for r in range(ROUNDS):
        lengths = lax.dynamic_index_in_dim(val_lengths, round_owner[r], 0, keepdims=False)
        seg = lax.dynamic_slice_in_dim(segment_of(lengths, val_rows), core * half, half, 0)
        hots.append((seg[:, None] == jnp.arange(128, dtype=jnp.int32)[None, :]).astype(jnp.float32))
        weights.append(
            1.0
            / math.sqrt(D * FF)
            / jnp.sqrt(
                cand_lengths[0].astype(jnp.float32)[:, None]
                * lengths.astype(jnp.float32)[None, :]
            )
        )
    partial = score(
        cand_hot, jnp.stack(hots, axis=0), parts["gu_h"], parts["x"], parts["dy"]
    )
    total = partial[:, :samples] + lax.ppermute(partial[:, samples:], "dp", across)
    turned = [
        lax.ppermute(total, "tensor", [(z, (z + m) % n_tensor) for z in range(n_tensor)])
        for m in range(1, n_tensor)
    ]
    for piece in turned:
        total = total + piece
    return total[:, :, : val_lengths.shape[1]] * jnp.stack(weights, axis=0)


def solution(mesh):
    n_dp, n_tensor = mesh.shape["dp"], mesh.shape["tensor"]
    in_specs = (P("dp", "tensor"),) * 10 + (P("dp", None), P(), P())
    return jax.shard_map(
        functools.partial(local, n_dp, n_tensor),
        mesh=mesh,
        in_specs=in_specs,
        out_specs=P(None, "dp", None),
        check_vma=False,
    )
```

```python
import functools
import math

import jax
import jax.numpy as jnp
from jax import lax
from jax.experimental import pallas as pl
from jax.experimental.pallas import tpu as pltpu
from jax.sharding import PartitionSpec as P

D = 8192
FF = 28672
ROUNDS = 2
FB = 896
W = 3 * FB
VMEM = 64 * 1024 * 1024 - 256 * 1024

NT = (((1,), (1,)), ((), ()))


def derive(gate, up, grad_hidden):
    gate_f = gate.astype(jnp.float32)
    up_f = up.astype(jnp.float32)
    grad_f = grad_hidden.astype(jnp.float32)
    sigmoid_gate = jax.nn.sigmoid(gate_f)
    activated = gate_f * sigmoid_gate
    hidden = (activated * up_f).astype(jnp.bfloat16)
    grad_gate = (grad_f * up_f * sigmoid_gate * (1.0 + gate_f * (1.0 - sigmoid_gate))).astype(
        jnp.bfloat16
    )
    grad_up = (grad_f * activated).astype(jnp.bfloat16)
    return (grad_gate, grad_up, hidden)


def segment_of(lengths, total):
    bounds = jnp.cumsum(lengths)
    position = jnp.arange(total, dtype=jnp.int32)
    return jnp.sum((position[:, None] >= bounds[None, :]).astype(jnp.int32), axis=1)


def segments(j, width):
    out = []
    for which in (0, 1):
        lo = max(j * W, which * width)
        hi = min((j + 1) * W, (which + 1) * width)
        if hi > lo:
            out.append((which, lo - which * width, lo - j * W, hi - lo))
    return out


ANYWHERE = pl.BlockSpec(memory_space=pl.ANY)
IN_HBM = pl.BlockSpec(memory_space=pltpu.HBM)
IN_SMEM = pl.BlockSpec(memory_space=pltpu.SMEM)
MARK = jax.ShapeDtypeStruct((8, 128), jnp.float32)


def place_of(chip, chips):
    return jnp.where(chip < chips // 2, chip, chips // 2 + chips - 1 - chip)


def away_of(me, owner, chips):
    behind = place_of(me // 2, chips) - place_of(owner // 2, chips)
    return lax.rem(jnp.where(me % 2 == 0, behind, -behind) + chips, chips)


def pack_body(groups, width, first, half, gate, up, dh, x, dy, *rest):
    out = rest[-2]
    k = pl.program_id(0) + first

    @pl.when(k < groups)
    def _():
        out[0, :, 0:FB] = gate[...]
        out[0, :, FB : 2 * FB] = up[...]
        out[0, :, 2 * FB : 3 * FB] = dh[...]

    for j in range(-(-2 * width // W)):

        @pl.when(k == groups + j)
        def _():
            end = 0
            for which, src, dst, cols in segments(j, width):
                out[0, :, dst : dst + cols] = (x, dy)[which][:, src : src + cols]
                end = dst + cols
            if end < W:
                out[0, :, end:W] = jnp.zeros((out.shape[1], W - end), out.dtype)


def pack(half, rows, first, count, deps, *arrays):
    groups, width = arrays[0].shape[1] // FB, arrays[3].shape[1]
    wide = pl.BlockSpec(
        (rows, FB), lambda k, half: (half[0], jnp.minimum(k + first, groups - 1))
    )
    flat = pl.BlockSpec((rows, width), lambda k, half: (half[0], 0))
    return pl.pallas_call(
        functools.partial(pack_body, groups, width, first),
        grid_spec=pltpu.PrefetchScalarGridSpec(
            num_scalar_prefetch=1,
            grid=(count,),
            in_specs=[wide, wide, wide, flat, flat] + [ANYWHERE] * len(deps),
            out_specs=[pl.BlockSpec((1, rows, W), lambda k, half: (k, 0, 0)), IN_HBM],
        ),
        out_shape=[jax.ShapeDtypeStruct((count, rows, W), jnp.bfloat16), MARK],
        cost_estimate=pl.CostEstimate(
            flops=0, bytes_accessed=4 * count * rows * W, transcendentals=0
        ),
        compiler_params=pltpu.CompilerParams(vmem_limit_bytes=VMEM),
    )(half, *arrays, *deps)


def inject_body(t, at, r, groups, width, n_dp, always, owner, gate, up, dh, x, dy, sib, *rest):
    out, room, sem = rest[-3:]
    rows = out.shape[0]
    if t >= groups + -(-2 * width // W):
        return
    me = lax.axis_index("dp")
    start = pl.multiple_of(me % 2 * rows, rows)
    mine = owner[r] % 2 == me % 2
    first = jnp.logical_or(always, owner[r] // 2 == me // 2)

    if t < groups:
        parts = [(ref, t * FB, i * FB, FB) for i, ref in enumerate((gate, up, dh))]
    else:
        parts = [
            ((x, dy)[which], src, dst, cols)
            for which, src, dst, cols in segments(t - groups, width)
        ]

    def through(sources):
        ins, outs = [], []
        half = rows // 2
        for n in (0, 1):
            some = pl.ds(n * half, half)
            for source, first, src, dst, cols in sources:
                there = room.at[some, pl.ds(dst, cols)]
                i = len(ins)
                here = source.at[pl.ds(first + n * half, half), pl.ds(src, cols)]
                ins.append(pltpu.make_async_copy(here, there, sem.at[0, i]))
                outs.append(
                    pltpu.make_async_copy(there, out.at[some, pl.ds(dst, cols)], sem.at[1, i])
                )
        for copy in ins:
            copy.start()
        for before, copy in zip(ins, outs):
            before.wait()
            copy.start()
        for copy in outs:
            copy.wait()

    @pl.when(first)
    def _():
        @pl.when(mine)
        def _():
            through([(ref, start, src, dst, cols) for ref, src, dst, cols in parts])

        @pl.when(jnp.logical_not(mine))
        def _():
            through([(sib.at[at], 0, dst, dst, cols) for _, _, dst, cols in parts])


def inject(t, at, r, rows, n_dp, owner, vals, sib, held, deps):
    groups, width = vals[0].shape[1] // FB, vals[3].shape[1]
    extra = ([] if held is None else [held]) + list(deps)
    return pl.pallas_call(
        functools.partial(inject_body, t, at, r, groups, width, n_dp, held is None),
        in_specs=[IN_SMEM]
        + [IN_HBM] * (6 if held is None else 7)
        + [ANYWHERE] * len(deps),
        out_specs=IN_HBM,
        out_shape=jax.ShapeDtypeStruct((rows, W), jnp.bfloat16),
        scratch_shapes=[pltpu.VMEM((rows, W), jnp.bfloat16), pltpu.SemaphoreType.DMA((2, 6))],
        input_output_aliases={} if held is None else {7: 0},
        cost_estimate=pl.CostEstimate(
            flops=0, bytes_accessed=4 * rows * W, transcendentals=0
        ),
        compiler_params=pltpu.CompilerParams(vmem_limit_bytes=VMEM),
    )(owner, *vals, sib, *extra)


def use_body(k, groups, width, chips, fresh, owner, own, sib, held, accs_in, accs, room, val, sums, sem):
    rows = room.shape[1]
    half = val.shape[0] // ROUNDS
    me = lax.axis_index("dp")
    brought = []
    for r in range(ROUNDS):
        away = away_of(me, owner[r], chips)
        there = val.at[pl.ds(r * half, half)]
        for i in range(chips):

            @pl.when(away == i)
            def _():
                pltpu.make_async_copy(held[r * chips + i], there, sem.at[r]).start()

        brought.append(pltpu.make_async_copy(held[r * chips], there, sem.at[r]))
    if k < groups:
        parts = [(i, k * FB, i * FB, FB) for i in range(3)]
    else:
        parts = [(3 + which, src, dst, cols) for which, src, dst, cols in segments(k - groups, width)]
    loads = []
    for side, arrays in enumerate((own, sib)):
        loads.append([])
        for i, (which, src, dst, cols) in enumerate(parts):
            copy = pltpu.make_async_copy(
                arrays[which].at[:, pl.ds(src, cols)],
                room.at[side, :, pl.ds(dst, cols)],
                sem.at[2 + 3 * side + i],
            )
            copy.start()
            loads[side].append(copy)
    priors, slot = [], 0
    slots = []
    for i, acc in enumerate(accs):
        n = acc.shape[0]
        slots.append((slot, n))
        if not fresh[i]:
            copy = pltpu.make_async_copy(accs_in.pop(0), sums.at[pl.ds(slot, n)], sem.at[8 + i])
            copy.start()
            priors.append(copy)
        slot += n

    def derive_in(ref):
        def some(i, carry):
            at = [pl.ds(pl.multiple_of(m * FB + i * 128, 128), 128) for m in range(3)]
            new = derive(ref[:, at[0]], ref[:, at[1]], ref[:, at[2]])
            for m in range(3):
                ref[:, at[m]] = new[m]
            return carry

        lax.fori_loop(0, FB // 128, some, 0)

    for copy in brought:
        copy.wait()
    if k < groups:
        derive_in(val)
    for copy in priors:
        copy.wait()
    stores = []
    for side in (0, 1):
        for copy in loads[side]:
            copy.wait()
        at = pl.ds(side * rows, rows)

        def dot(left, right):
            return lax.dot_general(left, right, NT, preferred_element_type=jnp.float32)

        if k < groups:
            derive_in(room.at[side])
            terms = [
                dot(room[side, :, a:b], val[:, a:b]) for a, b in ((0, 2 * FB), (2 * FB, 3 * FB))
            ]
        else:
            terms = [
                dot(room[side, :, dst : dst + cols], val[:, dst : dst + cols])
                for _, _, dst, cols in parts
            ]
        for i, term in enumerate(terms):
            if fresh[i if len(accs) > 1 else 0]:
                sums[i, at, :] = term
            else:
                sums[i, at, :] += term
        for i, acc in enumerate(accs):
            first, n = slots[i]
            copy = pltpu.make_async_copy(
                sums.at[pl.ds(first, n), at], acc.at[:, at], sem.at[10 + 2 * side + i]
            )
            copy.start()
            stores.append(copy)
    for copy in stores:
        copy.wait()


def use(k, owner, groups, width, chips, own, sib, held, grams, deps):
    cand_rows, half = own[0].shape[0], held[0].shape[0]
    if k < groups:
        names = [("gu_h", 2)]
    else:
        names = [(("x", "dy")[which], 1) for which, _, _, _ in segments(k - groups, width)]
    fresh = [name not in grams for name, _ in names]
    priors = [grams[name] for name, _ in names if name in grams]
    shapes = [
        jax.ShapeDtypeStruct((n, 2 * cand_rows, ROUNDS * half), jnp.float32) for _, n in names
    ]
    n_cand, n_held = len(own), len(held)

    def body(owner, *refs):
        a, b = n_cand, 2 * n_cand
        c = b + n_held
        d = c + len(priors)
        e = d + len(deps)
        f = e + len(shapes)
        use_body(
            k, groups, width, chips, fresh, owner, refs[:a], refs[a:b], refs[b:c],
            list(refs[c:d]), refs[e:f], *refs[f + 1 :],
        )

    results = pl.pallas_call(
        body,
        in_specs=[IN_SMEM]
        + [IN_HBM] * (2 * n_cand + n_held + len(priors))
        + [ANYWHERE] * len(deps),
        out_specs=[IN_HBM] * (len(shapes) + 1),
        out_shape=shapes + [MARK],
        scratch_shapes=[
            pltpu.VMEM((2, cand_rows, W), jnp.bfloat16),
            pltpu.VMEM((ROUNDS * half, W), jnp.bfloat16),
            pltpu.VMEM((2, 2 * cand_rows, ROUNDS * half), jnp.float32),
            pltpu.SemaphoreType.DMA((14,)),
        ],
        cost_estimate=pl.CostEstimate(
            flops=8 * cand_rows * half * W,
            bytes_accessed=4 * (cand_rows + half) * W + 32 * cand_rows * half,
            transcendentals=2 * (cand_rows + half) * FB,
        ),
        compiler_params=pltpu.CompilerParams(vmem_limit_bytes=VMEM),
    )(owner, *own, *sib, *held, *priors, *deps)
    for (name, _), value in zip(names, results):
        grams[name] = value
    return results[-1]


def cut_body(pieces, at, acc, own, *others):
    block = own.shape[1]
    for m in range(pieces):
        rows = pl.ds(pl.multiple_of(lax.rem(at[0] + m, pieces) * block, block), block)
        tile = acc[:, rows, :]
        if m == 0:
            own[...] = tile
        else:
            others[m - 1][...] = tile.astype(jnp.bfloat16)


def cut(at_z, pieces, acc):
    shape = (acc.shape[0], acc.shape[1] // pieces, acc.shape[2])
    whole = pl.BlockSpec(shape, lambda i, at: (0, 0, 0))
    return pl.pallas_call(
        functools.partial(cut_body, pieces),
        grid_spec=pltpu.PrefetchScalarGridSpec(
            num_scalar_prefetch=1,
            grid=(1,),
            in_specs=[pl.BlockSpec(acc.shape, lambda i, at: (0, 0, 0))],
            out_specs=[whole] * pieces,
        ),
        out_shape=[jax.ShapeDtypeStruct(shape, jnp.float32)]
        + [jax.ShapeDtypeStruct(shape, jnp.bfloat16)] * (pieces - 1),
        cost_estimate=pl.CostEstimate(flops=0, bytes_accessed=8 * acc.size, transcendentals=0),
        compiler_params=pltpu.CompilerParams(vmem_limit_bytes=VMEM),
    )(at_z[None], acc)


def score_body(pieces, cand_hot, val_hot, *refs):
    out = refs[-1]

    def total(i, slot):
        value = refs[i * pieces][slot]
        for ref in refs[i * pieces + 1 : (i + 1) * pieces]:
            value = value + ref[slot].astype(jnp.float32)
        return value

    pair = total(1, 0) * total(0, 0) + total(0, 1) * total(2, 0)
    half = pair.shape[1] // ROUNDS
    summed = jnp.dot(
        cand_hot[...],
        pair,
        precision=lax.Precision.HIGHEST,
        preferred_element_type=jnp.float32,
    )
    for r in range(ROUNDS):
        out[r] = jnp.dot(
            summed[:, r * half : (r + 1) * half],
            val_hot[r],
            precision=lax.Precision.HIGHEST,
            preferred_element_type=jnp.float32,
        )


def score(cand_hot, val_hot, gu_h, x, dy):
    return pl.pallas_call(
        functools.partial(score_body, len(x)),
        out_shape=jax.ShapeDtypeStruct(
            (ROUNDS, cand_hot.shape[0], val_hot.shape[2]), jnp.float32
        ),
        compiler_params=pltpu.CompilerParams(vmem_limit_bytes=VMEM),
    )(cand_hot, val_hot, *gu_h, *x, *dy)


def local(
    n_dp,
    n_tensor,
    cand_gate,
    cand_up,
    cand_dh,
    cand_x,
    cand_dy,
    val_gate,
    val_up,
    val_dh,
    val_x,
    val_dy,
    cand_lengths,
    val_lengths,
    round_owner,
):
    chips = n_dp // 2
    ring = list(range(chips // 2)) + list(range(chips - 1, chips // 2 - 1, -1))
    along = []
    for i, chip in enumerate(ring):
        along.append((2 * chip, 2 * ring[(i + 1) % chips]))
        along.append((2 * chip + 1, 2 * ring[(i - 1) % chips] + 1))
    across = [(i, i ^ 1) for i in range(n_dp)]

    at_z = lax.axis_index("tensor")
    core = lax.axis_index("dp") % 2

    cand_rows, val_rows = cand_x.shape[0], val_x.shape[0]
    half = val_rows // 2
    groups, width = cand_gate.shape[1] // FB, cand_x.shape[1]
    count = groups + -(-2 * width // W)
    vals = (val_gate, val_up, val_dh, val_x, val_dy)
    own = (cand_gate, cand_up, cand_dh, cand_x, cand_dy)
    other = (1 - core)[None]

    sib_parts = [None] * count

    def send_half(lo, hi, deps):
        part, mark = pack(other, half, lo, hi - lo, deps, *vals)
        part = lax.ppermute(part, "dp", across)
        for t in range(lo, hi):
            sib_parts[t] = (part, t - lo)
        return mark

    mark = send_half(0, 1, [])
    sib = [lax.ppermute(array, "dp", across) for array in own]
    sib_lengths = lax.ppermute(cand_lengths, "dp", across)

    grams, parts = {}, {}
    steps = count + chips - 1
    held = [[None] * steps for _ in range(ROUNDS)]
    got = [None] * ROUNDS

    def scatter(name):
        pieces = cut(at_z, n_tensor, grams[name])
        parts[name] = [pieces[0]] + [
            lax.ppermute(pieces[m], "tensor", [(z, (z + m) % n_tensor) for z in range(n_tensor)])
            for m in range(1, n_tensor)
        ]

    last_of = {"gu_h": groups - 1}
    for k in range(groups, count):
        for which, _, _, _ in segments(k - groups, width):
            last_of[("x", "dy")[which]] = k

    def consume(k, deps):
        came = [held[r][k + i] for r in range(ROUNDS) for i in range(chips)]
        mark = use(k, round_owner, groups, width, chips, own, sib, came, grams, deps)
        for name in last_of:
            if last_of[name] == k:
                scatter(name)
        return mark

    work = []
    cuts = [c for c in (1, 2, 3, 4, 6, 8, 9) if c < count] + [count]
    for lo, hi in zip(cuts[:-1], cuts[1:]):
        work.append((0, functools.partial(send_half, lo, hi)))
    for k in range(count):
        work.append(((k + chips) * ROUNDS - 1, functools.partial(consume, k)))

    slot = 0
    for t in range(steps):
        for r in range(ROUNDS):
            if t < steps - 1:
                part, at = sib_parts[min(t, count - 1)]
                held[r][t] = inject(t, at, r, half, n_dp, round_owner, vals, part, got[r], [mark])
            else:
                held[r][t] = got[r]
            if t < steps - 1:
                got[r] = lax.ppermute(held[r][t], "dp", along)
            if work and work[0][0] <= slot:
                mark = work.pop(0)[1]([held[r][t]])
            slot += 1
    while work:
        mark = work.pop(0)[1]([mark])

    block = 2 * cand_rows // n_tensor
    samples = cand_lengths.shape[1]
    segs = jnp.concatenate(
        [
            segment_of(cand_lengths[0], cand_rows),
            segment_of(sib_lengths[0], cand_rows) + samples,
        ]
    )
    segs = lax.dynamic_slice_in_dim(segs, at_z * block, block, 0)
    cand_hot = (jnp.arange(2 * samples, dtype=jnp.int32)[:, None] == segs[None, :]).astype(
        jnp.float32
    )
    hots, weights = [], []
    for r in range(ROUNDS):
        lengths = lax.dynamic_index_in_dim(val_lengths, round_owner[r], 0, keepdims=False)
        seg = lax.dynamic_slice_in_dim(segment_of(lengths, val_rows), core * half, half, 0)
        hots.append((seg[:, None] == jnp.arange(128, dtype=jnp.int32)[None, :]).astype(jnp.float32))
        weights.append(
            1.0
            / math.sqrt(D * FF)
            / jnp.sqrt(
                cand_lengths[0].astype(jnp.float32)[:, None]
                * lengths.astype(jnp.float32)[None, :]
            )
        )
    partial = score(
        cand_hot, jnp.stack(hots, axis=0), parts["gu_h"], parts["x"], parts["dy"]
    )
    total = partial[:, :samples] + lax.ppermute(partial[:, samples:], "dp", across)
    turned = [
        lax.ppermute(total, "tensor", [(z, (z + m) % n_tensor) for z in range(n_tensor)])
        for m in range(1, n_tensor)
    ]
    for piece in turned:
        total = total + piece
    return total[:, :, : val_lengths.shape[1]] * jnp.stack(weights, axis=0)


def solution(mesh):
    n_dp, n_tensor = mesh.shape["dp"], mesh.shape["tensor"]
    in_specs = (P("dp", "tensor"),) * 10 + (P("dp", None), P(), P())
    return jax.shard_map(
        functools.partial(local, n_dp, n_tensor),
        mesh=mesh,
        in_specs=in_specs,
        out_specs=P(None, "dp", None),
        check_vma=False,
    )
```

```python
import functools
import math

import jax
import jax.numpy as jnp
from jax import lax
from jax.experimental import pallas as pl
from jax.experimental.pallas import tpu as pltpu
from jax.sharding import PartitionSpec as P

D = 8192
FF = 28672
ROUNDS = 2
FB = 896
W = 3 * FB
VMEM = 64 * 1024 * 1024 - 256 * 1024

NT = (((1,), (1,)), ((), ()))


def derive(gate, up, grad_hidden):
    gate_f = gate.astype(jnp.float32)
    up_f = up.astype(jnp.float32)
    grad_f = grad_hidden.astype(jnp.float32)
    sigmoid_gate = jax.nn.sigmoid(gate_f)
    activated = gate_f * sigmoid_gate
    hidden = (activated * up_f).astype(jnp.bfloat16)
    grad_gate = (grad_f * up_f * sigmoid_gate * (1.0 + gate_f * (1.0 - sigmoid_gate))).astype(
        jnp.bfloat16
    )
    grad_up = (grad_f * activated).astype(jnp.bfloat16)
    return (grad_gate, grad_up, hidden)


def segments(j, width):
    out = []
    for which in (0, 1):
        lo = max(j * W, which * width)
        hi = min((j + 1) * W, (which + 1) * width)
        if hi > lo:
            out.append((which, lo - which * width, lo - j * W, hi - lo))
    return out


ANYWHERE = pl.BlockSpec(memory_space=pl.ANY)
IN_HBM = pl.BlockSpec(memory_space=pltpu.HBM)
IN_SMEM = pl.BlockSpec(memory_space=pltpu.SMEM)
MARK = jax.ShapeDtypeStruct((8, 128), jnp.float32)


def place_of(chip, chips):
    return jnp.where(chip < chips // 2, chip, chips // 2 + chips - 1 - chip)


def away_of(me, owner, chips):
    behind = place_of(me // 2, chips) - place_of(owner // 2, chips)
    return lax.rem(jnp.where(me % 2 == 0, behind, -behind) + chips, chips)


def valid(j, width):
    return max(dst + cols for _, _, dst, cols in segments(j, width))


def pack_body(groups, width, first, half, gate, up, dh, x, dy, *rest):
    out = rest[-2]
    k = pl.program_id(0) + first

    @pl.when(k < groups)
    def _():
        out[0, :, 0:FB] = gate[...]
        out[0, :, FB : 2 * FB] = up[...]
        out[0, :, 2 * FB : 3 * FB] = dh[...]

    for j in range(-(-2 * width // W)):

        @pl.when(k == groups + j)
        def _():
            end = 0
            for which, src, dst, cols in segments(j, width):
                out[0, :, dst : dst + cols] = (x, dy)[which][:, src : src + cols]
                end = dst + cols
            if end < W:
                out[0, :, end:W] = jnp.zeros((out.shape[1], W - end), out.dtype)


def pack(half, rows, first, count, deps, *arrays):
    groups, width = arrays[0].shape[1] // FB, arrays[3].shape[1]
    wide = pl.BlockSpec(
        (rows, FB), lambda k, half: (half[0], jnp.minimum(k + first, groups - 1))
    )
    flat = pl.BlockSpec((rows, width), lambda k, half: (half[0], 0))
    return pl.pallas_call(
        functools.partial(pack_body, groups, width, first),
        grid_spec=pltpu.PrefetchScalarGridSpec(
            num_scalar_prefetch=1,
            grid=(count,),
            in_specs=[wide, wide, wide, flat, flat] + [ANYWHERE] * len(deps),
            out_specs=[pl.BlockSpec((1, rows, W), lambda k, half: (k, 0, 0)), IN_HBM],
        ),
        out_shape=[jax.ShapeDtypeStruct((count, rows, W), jnp.bfloat16), MARK],
        cost_estimate=pl.CostEstimate(
            flops=16 * rows * rows * W, bytes_accessed=24 * rows * W, transcendentals=0
        ),
        compiler_params=pltpu.CompilerParams(vmem_limit_bytes=VMEM),
    )(half, *arrays, *deps)


def inject_body(t, at, r, groups, width, n_dp, always, owner, gate, up, dh, x, dy, sib, *rest):
    out, room, sem = rest[-3:]
    rows = out.shape[0]
    if t >= groups + -(-2 * width // W):
        return
    me = lax.axis_index("dp")
    start = pl.multiple_of(me % 2 * rows, rows)
    mine = owner[r] % 2 == me % 2
    first = jnp.logical_or(always, owner[r] // 2 == me // 2)

    if t < groups:
        parts = [(ref, t * FB, i * FB, FB) for i, ref in enumerate((gate, up, dh))]
    else:
        parts = [
            ((x, dy)[which], src, dst, cols)
            for which, src, dst, cols in segments(t - groups, width)
        ]

    def through(sources):
        ins, outs = [], []
        half = rows // 2
        for n in (0, 1):
            some = pl.ds(n * half, half)
            for source, first, src, dst, cols in sources:
                there = room.at[some, pl.ds(dst, cols)]
                i = len(ins)
                here = source.at[pl.ds(first + n * half, half), pl.ds(src, cols)]
                ins.append(pltpu.make_async_copy(here, there, sem.at[0, i]))
                outs.append(
                    pltpu.make_async_copy(there, out.at[some, pl.ds(dst, cols)], sem.at[1, i])
                )
        for copy in ins:
            copy.start()
        for before, copy in zip(ins, outs):
            before.wait()
            copy.start()
        for copy in outs:
            copy.wait()

    @pl.when(first)
    def _():
        @pl.when(mine)
        def _():
            through([(ref, start, src, dst, cols) for ref, src, dst, cols in parts])

        @pl.when(jnp.logical_not(mine))
        def _():
            through([(sib.at[at], 0, dst, dst, cols) for _, _, dst, cols in parts])


def inject(t, at, r, rows, n_dp, owner, vals, sib, held, deps):
    groups, width = vals[0].shape[1] // FB, vals[3].shape[1]
    extra = ([] if held is None else [held]) + list(deps)
    return pl.pallas_call(
        functools.partial(inject_body, t, at, r, groups, width, n_dp, held is None),
        in_specs=[IN_SMEM]
        + [IN_HBM] * (6 if held is None else 7)
        + [ANYWHERE] * len(deps),
        out_specs=IN_HBM,
        out_shape=jax.ShapeDtypeStruct((rows, W), jnp.bfloat16),
        scratch_shapes=[pltpu.VMEM((rows, W), jnp.bfloat16), pltpu.SemaphoreType.DMA((2, 6))],
        input_output_aliases={} if held is None else {7: 0},
        cost_estimate=pl.CostEstimate(
            flops=0, bytes_accessed=4 * rows * W, transcendentals=0
        ),
        compiler_params=pltpu.CompilerParams(vmem_limit_bytes=VMEM),
    )(owner, *vals, sib, *extra)


def trim_body(source, *rest):
    out, room, sem = rest[-3:]
    rows, cols = out.shape
    some = rows // 4
    ins, outs = [], []
    for i in range(4):
        at = pl.ds(i * some, some)
        ins.append(
            pltpu.make_async_copy(source.at[at, pl.ds(0, cols)], room.at[at], sem.at[0, i])
        )
        outs.append(pltpu.make_async_copy(room.at[at], out.at[at], sem.at[1, i]))
    for copy in ins:
        copy.start()
    for before, copy in zip(ins, outs):
        before.wait()
        copy.start()
    for copy in outs:
        copy.wait()


def trim(source, cols, deps):
    rows = source.shape[0]
    return pl.pallas_call(
        trim_body,
        in_specs=[IN_HBM] + [ANYWHERE] * len(deps),
        out_specs=IN_HBM,
        out_shape=jax.ShapeDtypeStruct((rows, cols), source.dtype),
        scratch_shapes=[pltpu.VMEM((rows, cols), source.dtype), pltpu.SemaphoreType.DMA((2, 4))],
        cost_estimate=pl.CostEstimate(flops=0, bytes_accessed=4 * rows * cols, transcendentals=0),
        compiler_params=pltpu.CompilerParams(vmem_limit_bytes=VMEM),
    )(source, *deps)


def use_body(k, groups, width, chips, names, fresh, owner, own, sib, held, accs_in, accs, room, val, sums, sem):
    rows = room.shape[1]
    half = val.shape[0] // ROUNDS
    me = lax.axis_index("dp")
    brought = []
    for r in range(ROUNDS):
        away = away_of(me, owner[r], chips)
        cols = 3 * FB if k < groups else valid(k - groups, width)
        there = val.at[pl.ds(r * half, half), pl.ds(0, cols)]
        for i in range(chips):

            @pl.when(away == i)
            def _():
                pltpu.make_async_copy(
                    held[r * chips + i].at[:, pl.ds(0, cols)], there, sem.at[r]
                ).start()

        brought.append(
            pltpu.make_async_copy(held[r * chips].at[:, pl.ds(0, cols)], there, sem.at[r])
        )
    if k < groups:
        parts = [(i, k * FB, i * FB, FB) for i in range(3)]
    else:
        parts = segments(k - groups, width)
    loads = []
    for side, arrays in enumerate((own, sib)):
        loads.append([])
        for i, (which, src, dst, cols) in enumerate(parts):
            copy = pltpu.make_async_copy(
                arrays[which].at[:, pl.ds(src, cols)],
                room.at[side, :, pl.ds(dst, cols)],
                sem.at[2 + 3 * side + i],
            )
            copy.start()
            loads[side].append(copy)
    priors, slot = [], 0
    slots = []
    for i, (_, n, _) in enumerate(names):
        slots.append((slot, n))
        if not fresh[i]:
            copy = pltpu.make_async_copy(accs_in.pop(0), sums.at[pl.ds(slot, n)], sem.at[8 + i])
            copy.start()
            priors.append(copy)
        slot += n

    def derive_in(ref):
        def some(i, carry):
            at = [pl.ds(pl.multiple_of(m * FB + i * 128, 128), 128) for m in range(3)]
            new = derive(ref[:, at[0]], ref[:, at[1]], ref[:, at[2]])
            for m in range(3):
                ref[:, at[m]] = new[m]
            return carry

        lax.fori_loop(0, FB // 128, some, 0)

    for copy in brought:
        copy.wait()
    if k < groups:
        derive_in(val)
    for copy in priors:
        copy.wait()
    stores = []
    for side in (0, 1):
        for copy in loads[side]:
            copy.wait()
        at = pl.ds(side * rows, rows)

        def dot(left, right):
            return lax.dot_general(left, right, NT, preferred_element_type=jnp.float32)

        if k < groups:
            derive_in(room.at[side])
            terms = [
                dot(room[side, :, a:b], val[:, a:b]) for a, b in ((0, 2 * FB), (2 * FB, 3 * FB))
            ]
        else:
            terms = [
                dot(room[side, :, dst : dst + cols], val[:, dst : dst + cols])
                for _, _, dst, cols in parts
            ]
        for i, term in enumerate(terms):
            if fresh[i if len(names) > 1 else 0]:
                sums[i, at, :] = term
            else:
                sums[i, at, :] += term
        for i, (_, _, pieces) in enumerate(names):
            if pieces == 0:
                first, n = slots[i]
                copy = pltpu.make_async_copy(
                    sums.at[pl.ds(first, n), at], accs[i][0].at[:, at], sem.at[10 + 2 * side + i]
                )
                copy.start()
                stores.append(copy)
    for i, (_, _, pieces) in enumerate(names):
        first, n = slots[i]
        for m in range(pieces):
            out = accs[i][m]
            block = out.shape[1]
            at = pl.multiple_of(lax.rem(lax.axis_index("tensor") + m, pieces) * block, block)
            out[...] = sums[first : first + n, pl.ds(at, block), :].astype(out.dtype)
    for copy in stores:
        copy.wait()


def use(k, owner, groups, width, chips, n_tensor, own, sib, held, grams, deps):
    cand_rows, half = own[0].shape[0], held[0].shape[0]
    if k < groups:
        names = [("gu_h", 2, n_tensor if k == groups - 1 else 0)]
    else:
        names = [
            (("x", "dy")[which], 1, n_tensor if src + cols == width else 0)
            for which, src, _, cols in segments(k - groups, width)
        ]
    fresh = [name not in grams for name, _, _ in names]
    priors = [grams[name] for name, _, _ in names if name in grams]
    shapes, places, cuts = [], [], []
    for _, n, pieces in names:
        rows = 2 * cand_rows // max(pieces, 1)
        cuts.append(len(shapes))
        for m in range(max(pieces, 1)):
            dtype = jnp.bfloat16 if m else jnp.float32
            shapes.append(jax.ShapeDtypeStruct((n, rows, ROUNDS * half), dtype))
            places.append(pl.BlockSpec(memory_space=pltpu.VMEM) if pieces else IN_HBM)
    cuts.append(len(shapes))
    n_cand, n_held = len(own), len(held)

    def body(owner, *refs):
        a, b = n_cand, 2 * n_cand
        c = b + n_held
        d = c + len(priors)
        e = d + len(deps)
        f = e + len(shapes)
        accs = [refs[e + i : e + j] for i, j in zip(cuts[:-1], cuts[1:])]
        use_body(
            k, groups, width, chips, names, fresh, owner, refs[:a], refs[a:b], refs[b:c],
            list(refs[c:d]), accs, *refs[f + 1 :],
        )

    results = pl.pallas_call(
        body,
        in_specs=[IN_SMEM]
        + [IN_HBM] * (2 * n_cand + n_held + len(priors))
        + [ANYWHERE] * len(deps),
        out_specs=places + [IN_HBM],
        out_shape=shapes + [MARK],
        scratch_shapes=[
            pltpu.VMEM((2, cand_rows, W), jnp.bfloat16),
            pltpu.VMEM((ROUNDS * half, W), jnp.bfloat16),
            pltpu.VMEM((2, 2 * cand_rows, ROUNDS * half), jnp.float32),
            pltpu.SemaphoreType.DMA((14,)),
        ],
        cost_estimate=pl.CostEstimate(
            flops=8 * cand_rows * half * W,
            bytes_accessed=4 * (cand_rows + half) * W + 32 * cand_rows * half,
            transcendentals=2 * (cand_rows + half) * FB,
        ),
        compiler_params=pltpu.CompilerParams(vmem_limit_bytes=VMEM),
    )(owner, *own, *sib, *held, *priors, *deps)
    done = {}
    for (name, _, pieces), i, j in zip(names, cuts[:-1], cuts[1:]):
        if pieces:
            done[name] = results[i:j]
        else:
            grams[name] = results[i]
    return results[-1], done


def score_body(pieces, cand_rows, own_len, sib_len, val_len, owner, *refs):
    mine, other = refs[-2:]

    def total(i, slot):
        value = refs[i * pieces][slot]
        for ref in refs[i * pieces + 1 : (i + 1) * pieces]:
            value = value + ref[slot].astype(jnp.float32)
        return value

    pair = total(1, 0) * total(0, 0) + total(0, 1) * total(2, 0)
    block, half = pair.shape[0], pair.shape[1] // ROUNDS
    samples, lanes = own_len.shape[1], mine.shape[2]

    row = lax.broadcasted_iota(jnp.int32, (2 * samples, block), 0)
    token = lax.axis_index("tensor") * block + lax.broadcasted_iota(
        jnp.int32, (2 * samples, block), 1
    )
    count_row = lax.broadcasted_iota(jnp.int32, (2 * samples, lanes), 0)
    cand_hot = jnp.zeros((2 * samples, block), jnp.float32)
    cand_count = jnp.ones((2 * samples, lanes), jnp.float32)
    for side, lengths in enumerate((own_len, sib_len)):
        low = jnp.int32(side * cand_rows)
        for i in range(samples):
            n = lengths[0, i]
            at = side * samples + i
            inside = (row == at) & (token >= low) & (token < low + n)
            cand_hot = jnp.where(inside, 1.0, cand_hot)
            cand_count = jnp.where(count_row == at, n.astype(jnp.float32), cand_count)
            low = low + n
    summed = jnp.dot(
        cand_hot,
        pair,
        precision=lax.Precision.HIGHEST,
        preferred_element_type=jnp.float32,
    )
    val_token = (lax.axis_index("dp") % 2) * half + lax.broadcasted_iota(
        jnp.int32, (half, lanes), 0
    )
    column = lax.broadcasted_iota(jnp.int32, (half, lanes), 1)
    count_column = lax.broadcasted_iota(jnp.int32, (2 * samples, lanes), 1)
    for r in range(ROUNDS):
        val_hot = jnp.zeros((half, lanes), jnp.float32)
        val_count = jnp.ones((2 * samples, lanes), jnp.float32)
        low = jnp.int32(0)
        for j in range(val_len.shape[1]):
            n = val_len[owner[r], j]
            inside = (column == j) & (val_token >= low) & (val_token < low + n)
            val_hot = jnp.where(inside, 1.0, val_hot)
            val_count = jnp.where(count_column == j, n.astype(jnp.float32), val_count)
            low = low + n
        scored = jnp.dot(
            summed[:, r * half : (r + 1) * half],
            val_hot,
            precision=lax.Precision.HIGHEST,
            preferred_element_type=jnp.float32,
        )
        scored = scored * (1.0 / math.sqrt(D * FF)) / jnp.sqrt(cand_count * val_count)
        mine[r] = scored[:samples]
        other[r] = scored[samples:]


def score(cand_rows, own_len, sib_len, val_len, owner, gu_h, x, dy):
    shape = jax.ShapeDtypeStruct((ROUNDS, own_len.shape[1], 128), jnp.float32)
    tiles = list(gu_h) + list(x) + list(dy)
    return pl.pallas_call(
        functools.partial(score_body, len(x), cand_rows),
        in_specs=[IN_SMEM] * 4 + [pl.BlockSpec(memory_space=pltpu.VMEM)] * len(tiles),
        out_shape=[shape, shape],
        compiler_params=pltpu.CompilerParams(vmem_limit_bytes=VMEM),
    )(own_len, sib_len, val_len, owner, *tiles)


def local(
    n_dp,
    n_tensor,
    cand_gate,
    cand_up,
    cand_dh,
    cand_x,
    cand_dy,
    val_gate,
    val_up,
    val_dh,
    val_x,
    val_dy,
    cand_lengths,
    val_lengths,
    round_owner,
):
    chips = n_dp // 2
    ring = list(range(chips // 2)) + list(range(chips - 1, chips // 2 - 1, -1))
    along = []
    for i, chip in enumerate(ring):
        along.append((2 * chip, 2 * ring[(i + 1) % chips]))
        along.append((2 * chip + 1, 2 * ring[(i - 1) % chips] + 1))
    across = [(i, i ^ 1) for i in range(n_dp)]

    core = lax.axis_index("dp") % 2

    cand_rows, val_rows = cand_x.shape[0], val_x.shape[0]
    half = val_rows // 2
    groups, width = cand_gate.shape[1] // FB, cand_x.shape[1]
    count = groups + -(-2 * width // W)
    vals = (val_gate, val_up, val_dh, val_x, val_dy)
    own = (cand_gate, cand_up, cand_dh, cand_x, cand_dy)
    other = (1 - core)[None]

    sib_parts = [None] * count

    def send_half(lo, hi, deps):
        part, mark = pack(other, half, lo, hi - lo, deps, *vals)
        part = lax.ppermute(part, "dp", across)
        for t in range(lo, hi):
            sib_parts[t] = (part, t - lo)
        return mark

    mark = send_half(0, 1, [])
    sib = []

    def send_next(deps):
        array = own[len(sib)]
        array = lax.optimization_barrier((array, *deps, *sib[-1:]))[0]
        sib.append(lax.ppermute(array, "dp", across))

    sib_lengths = lax.ppermute(cand_lengths, "dp", across)

    grams, parts = {}, {}
    steps = count + chips - 1
    held = [[None] * steps for _ in range(ROUNDS)]
    got = [None] * ROUNDS

    def consume(k, deps):
        came = [held[r][k + i] for r in range(ROUNDS) for i in range(chips)]
        kind = slice(0, 3) if k < groups else slice(3, 5)
        mark, done = use(
            k, round_owner, groups, width, chips, n_tensor, own[kind], sib[kind], came, grams, deps
        )
        for name, pieces in done.items():
            parts[name] = [pieces[0]] + [
                lax.ppermute(
                    pieces[m], "tensor", [(z, (z + m) % n_tensor) for z in range(n_tensor)]
                )
                for m in range(1, n_tensor)
            ]
        return mark

    work = []
    cuts = [c for c in (1, 2, 3, 4, 6, 8, 9) if c < count] + [count]
    for lo, hi in zip(cuts[:-1], cuts[1:]):
        work.append((1, functools.partial(send_half, lo, hi)))
    for k in range(count):
        work.append(((k + chips) * ROUNDS - 1, functools.partial(consume, k)))

    def latest(t, r):
        return [held[q][t] if q <= r else held[q][t - 1] for q in range(ROUNDS)]

    slot = 0
    for t in range(steps):
        for r in range(ROUNDS):
            if t < steps - 2:
                part, at = sib_parts[min(t, count - 1)]
                held[r][t] = inject(t, at, r, half, n_dp, round_owner, vals, part, got[r], [mark])
            else:
                held[r][t] = got[r]
            if t < steps - 2:
                got[r] = lax.ppermute(held[r][t], "dp", along)
            elif t == steps - 2:
                last = trim(held[r][t], valid(count - 1 - groups, width), [mark])
                got[r] = lax.ppermute(last, "dp", along)
            if slot in (0, 2, 4, 9, 13):
                send_next(latest(t, r))
            if work and work[0][0] <= slot:
                mark = work.pop(0)[1](latest(t, r))
            slot += 1
    while work:
        mark = work.pop(0)[1]([mark])

    mine, theirs = score(
        cand_rows, cand_lengths, sib_lengths, val_lengths, round_owner,
        parts["gu_h"], parts["x"], parts["dy"],
    )
    total = mine + lax.ppermute(theirs, "dp", across)
    turned = [
        lax.ppermute(total, "tensor", [(z, (z + m) % n_tensor) for z in range(n_tensor)])
        for m in range(1, n_tensor)
    ]
    for piece in turned:
        total = total + piece
    return total[:, :, : val_lengths.shape[1]]


def solution(mesh):
    n_dp, n_tensor = mesh.shape["dp"], mesh.shape["tensor"]
    in_specs = (P("dp", "tensor"),) * 10 + (P("dp", None), P(), P())
    return jax.shard_map(
        functools.partial(local, n_dp, n_tensor),
        mesh=mesh,
        in_specs=in_specs,
        out_specs=P(None, "dp", None),
        check_vma=False,
    )
```

```python
import functools
import math

import jax
import jax.numpy as jnp
from jax import lax
from jax.experimental import pallas as pl
from jax.experimental.pallas import tpu as pltpu
from jax.sharding import PartitionSpec as P

D = 8192
FF = 28672
ROUNDS = 2
FB = 896
W = 3 * FB
VMEM = 64 * 1024 * 1024 - 256 * 1024

NT = (((1,), (1,)), ((), ()))


def derive(gate, up, grad_hidden):
    gate_f = gate.astype(jnp.float32)
    up_f = up.astype(jnp.float32)
    grad_f = grad_hidden.astype(jnp.float32)
    sigmoid_gate = jax.nn.sigmoid(gate_f)
    activated = gate_f * sigmoid_gate
    hidden = (activated * up_f).astype(jnp.bfloat16)
    grad_gate = (grad_f * up_f * sigmoid_gate * (1.0 + gate_f * (1.0 - sigmoid_gate))).astype(
        jnp.bfloat16
    )
    grad_up = (grad_f * activated).astype(jnp.bfloat16)
    return (grad_gate, grad_up, hidden)


def segments(j, width):
    out = []
    for which in (0, 1):
        lo = max(j * W, which * width)
        hi = min((j + 1) * W, (which + 1) * width)
        if hi > lo:
            out.append((which, lo - which * width, lo - j * W, hi - lo))
    return out


ANYWHERE = pl.BlockSpec(memory_space=pl.ANY)
IN_HBM = pl.BlockSpec(memory_space=pltpu.HBM)
IN_SMEM = pl.BlockSpec(memory_space=pltpu.SMEM)
MARK = jax.ShapeDtypeStruct((8, 128), jnp.float32)


def place_of(chip, chips):
    return jnp.where(chip < chips // 2, chip, chips // 2 + chips - 1 - chip)


def away_of(me, owner, chips):
    behind = place_of(me // 2, chips) - place_of(owner // 2, chips)
    return lax.rem(jnp.where(me % 2 == 0, behind, -behind) + chips, chips)


def valid(j, width):
    return max(dst + cols for _, _, dst, cols in segments(j, width))


def pack_body(groups, width, first, half, gate, up, dh, x, dy, *rest):
    out = rest[-2]
    k = pl.program_id(0) + first

    @pl.when(k < groups)
    def _():
        out[0, :, 0:FB] = gate[...]
        out[0, :, FB : 2 * FB] = up[...]
        out[0, :, 2 * FB : 3 * FB] = dh[...]

    for j in range(-(-2 * width // W)):

        @pl.when(k == groups + j)
        def _():
            end = 0
            for which, src, dst, cols in segments(j, width):
                out[0, :, dst : dst + cols] = (x, dy)[which][:, src : src + cols]
                end = dst + cols
            if end < W:
                out[0, :, end:W] = jnp.zeros((out.shape[1], W - end), out.dtype)


def pack(half, rows, first, count, deps, *arrays):
    groups, width = arrays[0].shape[1] // FB, arrays[3].shape[1]
    wide = pl.BlockSpec(
        (rows, FB), lambda k, half: (half[0], jnp.minimum(k + first, groups - 1))
    )
    flat = pl.BlockSpec((rows, width), lambda k, half: (half[0], 0))
    return pl.pallas_call(
        functools.partial(pack_body, groups, width, first),
        grid_spec=pltpu.PrefetchScalarGridSpec(
            num_scalar_prefetch=1,
            grid=(count,),
            in_specs=[wide, wide, wide, flat, flat] + [ANYWHERE] * len(deps),
            out_specs=[pl.BlockSpec((1, rows, W), lambda k, half: (k, 0, 0)), IN_HBM],
        ),
        out_shape=[jax.ShapeDtypeStruct((count, rows, W), jnp.bfloat16), MARK],
        cost_estimate=pl.CostEstimate(
            flops=16 * rows * rows * W, bytes_accessed=24 * rows * W, transcendentals=0
        ),
        compiler_params=pltpu.CompilerParams(vmem_limit_bytes=VMEM),
    )(half, *arrays, *deps)


def inject_body(t, at, r, groups, width, n_dp, always, owner, gate, up, dh, x, dy, sib, *rest):
    out, room, sem = rest[-3:]
    rows = out.shape[0]
    if t >= groups + -(-2 * width // W):
        return
    me = lax.axis_index("dp")
    start = pl.multiple_of(me % 2 * rows, rows)
    mine = owner[r] % 2 == me % 2
    first = jnp.logical_or(always, owner[r] // 2 == me // 2)

    if t < groups:
        parts = [(ref, t * FB, i * FB, FB) for i, ref in enumerate((gate, up, dh))]
    else:
        parts = [
            ((x, dy)[which], src, dst, cols)
            for which, src, dst, cols in segments(t - groups, width)
        ]

    def through(sources):
        ins, outs = [], []
        half = rows // 2
        for n in (0, 1):
            some = pl.ds(n * half, half)
            for source, first, src, dst, cols in sources:
                there = room.at[some, pl.ds(dst, cols)]
                i = len(ins)
                here = source.at[pl.ds(first + n * half, half), pl.ds(src, cols)]
                ins.append(pltpu.make_async_copy(here, there, sem.at[0, i]))
                outs.append(
                    pltpu.make_async_copy(there, out.at[some, pl.ds(dst, cols)], sem.at[1, i])
                )
        for copy in ins:
            copy.start()
        for before, copy in zip(ins, outs):
            before.wait()
            copy.start()
        for copy in outs:
            copy.wait()

    @pl.when(first)
    def _():
        @pl.when(mine)
        def _():
            through([(ref, start, src, dst, cols) for ref, src, dst, cols in parts])

        @pl.when(jnp.logical_not(mine))
        def _():
            through([(sib.at[at], 0, dst, dst, cols) for _, _, dst, cols in parts])


def inject(t, at, r, rows, n_dp, owner, vals, sib, held, deps):
    groups, width = vals[0].shape[1] // FB, vals[3].shape[1]
    extra = ([] if held is None else [held]) + list(deps)
    return pl.pallas_call(
        functools.partial(inject_body, t, at, r, groups, width, n_dp, held is None),
        in_specs=[IN_SMEM]
        + [IN_HBM] * (6 if held is None else 7)
        + [ANYWHERE] * len(deps),
        out_specs=IN_HBM,
        out_shape=jax.ShapeDtypeStruct((rows, W), jnp.bfloat16),
        scratch_shapes=[pltpu.VMEM((rows, W), jnp.bfloat16), pltpu.SemaphoreType.DMA((2, 6))],
        input_output_aliases={} if held is None else {7: 0},
        cost_estimate=pl.CostEstimate(
            flops=0, bytes_accessed=4 * rows * W, transcendentals=0
        ),
        compiler_params=pltpu.CompilerParams(vmem_limit_bytes=VMEM),
    )(owner, *vals, sib, *extra)


def trim_body(source, *rest):
    out, room, sem = rest[-3:]
    rows, cols = out.shape
    some = rows // 4
    ins, outs = [], []
    for i in range(4):
        at = pl.ds(i * some, some)
        ins.append(
            pltpu.make_async_copy(source.at[at, pl.ds(0, cols)], room.at[at], sem.at[0, i])
        )
        outs.append(pltpu.make_async_copy(room.at[at], out.at[at], sem.at[1, i]))
    for copy in ins:
        copy.start()
    for before, copy in zip(ins, outs):
        before.wait()
        copy.start()
    for copy in outs:
        copy.wait()


def trim(source, cols, deps):
    rows = source.shape[0]
    return pl.pallas_call(
        trim_body,
        in_specs=[IN_HBM] + [ANYWHERE] * len(deps),
        out_specs=IN_HBM,
        out_shape=jax.ShapeDtypeStruct((rows, cols), source.dtype),
        scratch_shapes=[pltpu.VMEM((rows, cols), source.dtype), pltpu.SemaphoreType.DMA((2, 4))],
        cost_estimate=pl.CostEstimate(flops=0, bytes_accessed=4 * rows * cols, transcendentals=0),
        compiler_params=pltpu.CompilerParams(vmem_limit_bytes=VMEM),
    )(source, *deps)


def use_body(k, groups, width, chips, names, fresh, owner, own, sib, held, accs_in, accs, room, val, sums, sem):
    rows = room.shape[1]
    half = val.shape[0] // ROUNDS
    me = lax.axis_index("dp")
    brought = []
    for r in range(ROUNDS):
        away = away_of(me, owner[r], chips)
        cols = 3 * FB if k < groups else valid(k - groups, width)
        there = val.at[pl.ds(r * half, half), pl.ds(0, cols)]
        for i in range(chips):

            @pl.when(away == i)
            def _():
                pltpu.make_async_copy(
                    held[r * chips + i].at[:, pl.ds(0, cols)], there, sem.at[r]
                ).start()

        brought.append(
            pltpu.make_async_copy(held[r * chips].at[:, pl.ds(0, cols)], there, sem.at[r])
        )
    if k < groups:
        parts = [(i, k * FB, i * FB, FB) for i in range(3)]
    else:
        parts = segments(k - groups, width)
    loads = []
    for side, arrays in enumerate((own, sib)):
        loads.append([])
        for i, (which, src, dst, cols) in enumerate(parts):
            copy = pltpu.make_async_copy(
                arrays[which].at[:, pl.ds(src, cols)],
                room.at[side, :, pl.ds(dst, cols)],
                sem.at[2 + 3 * side + i],
            )
            copy.start()
            loads[side].append(copy)
    priors, slot = [], 0
    slots = []
    for i, (_, n, _) in enumerate(names):
        slots.append((slot, n))
        if not fresh[i]:
            copy = pltpu.make_async_copy(accs_in.pop(0), sums.at[pl.ds(slot, n)], sem.at[8 + i])
            copy.start()
            priors.append(copy)
        slot += n

    def derive_in(ref):
        def some(i, carry):
            at = [pl.ds(pl.multiple_of(m * FB + i * 128, 128), 128) for m in range(3)]
            new = derive(ref[:, at[0]], ref[:, at[1]], ref[:, at[2]])
            for m in range(3):
                ref[:, at[m]] = new[m]
            return carry

        lax.fori_loop(0, FB // 128, some, 0)

    for copy in brought:
        copy.wait()
    if k < groups:
        derive_in(val)
    for copy in priors:
        copy.wait()
    stores = []
    for side in (0, 1):
        for copy in loads[side]:
            copy.wait()
        at = pl.ds(side * rows, rows)

        def dot(left, right):
            return lax.dot_general(left, right, NT, preferred_element_type=jnp.float32)

        if k < groups:
            derive_in(room.at[side])
            terms = [
                dot(room[side, :, a:b], val[:, a:b]) for a, b in ((0, 2 * FB), (2 * FB, 3 * FB))
            ]
        else:
            terms = [
                dot(room[side, :, dst : dst + cols], val[:, dst : dst + cols])
                for _, _, dst, cols in parts
            ]
        for i, term in enumerate(terms):
            if fresh[i if len(names) > 1 else 0]:
                sums[i, at, :] = term
            else:
                sums[i, at, :] += term
        for i, (_, _, pieces) in enumerate(names):
            if pieces == 0:
                first, n = slots[i]
                copy = pltpu.make_async_copy(
                    sums.at[pl.ds(first, n), at], accs[i][0].at[:, at], sem.at[10 + 2 * side + i]
                )
                copy.start()
                stores.append(copy)
    for i, (_, _, pieces) in enumerate(names):
        first, n = slots[i]
        for m in range(pieces):
            out = accs[i][m]
            block = out.shape[1]
            at = pl.multiple_of(lax.rem(lax.axis_index("tensor") + m, pieces) * block, block)
            out[...] = sums[first : first + n, pl.ds(at, block), :].astype(out.dtype)
    for copy in stores:
        copy.wait()


def use(k, owner, groups, width, chips, n_tensor, own, sib, held, grams, deps):
    cand_rows, half = own[0].shape[0], held[0].shape[0]
    if k < groups:
        names = [("gu_h", 2, n_tensor if k == groups - 1 else 0)]
    else:
        names = [
            (("x", "dy")[which], 1, n_tensor if src + cols == width else 0)
            for which, src, _, cols in segments(k - groups, width)
        ]
    fresh = [name not in grams for name, _, _ in names]
    priors = [grams[name] for name, _, _ in names if name in grams]
    shapes, places, cuts = [], [], []
    for _, n, pieces in names:
        rows = 2 * cand_rows // max(pieces, 1)
        cuts.append(len(shapes))
        for m in range(max(pieces, 1)):
            dtype = jnp.bfloat16 if m else jnp.float32
            shapes.append(jax.ShapeDtypeStruct((n, rows, ROUNDS * half), dtype))
            places.append(pl.BlockSpec(memory_space=pltpu.VMEM) if pieces else IN_HBM)
    cuts.append(len(shapes))
    n_cand, n_held = len(own), len(held)

    def body(owner, *refs):
        a, b = n_cand, 2 * n_cand
        c = b + n_held
        d = c + len(priors)
        e = d + len(deps)
        f = e + len(shapes)
        accs = [refs[e + i : e + j] for i, j in zip(cuts[:-1], cuts[1:])]
        use_body(
            k, groups, width, chips, names, fresh, owner, refs[:a], refs[a:b], refs[b:c],
            list(refs[c:d]), accs, *refs[f + 1 :],
        )

    results = pl.pallas_call(
        body,
        in_specs=[IN_SMEM]
        + [IN_HBM] * (2 * n_cand + n_held + len(priors))
        + [ANYWHERE] * len(deps),
        out_specs=places + [IN_HBM],
        out_shape=shapes + [MARK],
        scratch_shapes=[
            pltpu.VMEM((2, cand_rows, W), jnp.bfloat16),
            pltpu.VMEM((ROUNDS * half, W), jnp.bfloat16),
            pltpu.VMEM((2, 2 * cand_rows, ROUNDS * half), jnp.float32),
            pltpu.SemaphoreType.DMA((14,)),
        ],
        cost_estimate=pl.CostEstimate(
            flops=8 * cand_rows * half * W,
            bytes_accessed=4 * (cand_rows + half) * W + 32 * cand_rows * half,
            transcendentals=2 * (cand_rows + half) * FB,
        ),
        compiler_params=pltpu.CompilerParams(vmem_limit_bytes=VMEM),
    )(owner, *own, *sib, *held, *priors, *deps)
    done = {}
    for (name, _, pieces), i, j in zip(names, cuts[:-1], cuts[1:]):
        if pieces:
            done[name] = results[i:j]
        else:
            grams[name] = results[i]
    return results[-1], done


def score_body(pieces, cand_rows, own_len, sib_len, val_len, owner, *refs):
    mine, other = refs[-2:]

    def total(i, slot):
        value = refs[i * pieces][slot]
        for ref in refs[i * pieces + 1 : (i + 1) * pieces]:
            value = value + ref[slot].astype(jnp.float32)
        return value

    pair = total(1, 0) * total(0, 0) + total(0, 1) * total(2, 0)
    block, half = pair.shape[0], pair.shape[1] // ROUNDS
    samples, lanes = own_len.shape[1], mine.shape[2]

    row = lax.broadcasted_iota(jnp.int32, (2 * samples, block), 0)
    token = lax.axis_index("tensor") * block + lax.broadcasted_iota(
        jnp.int32, (2 * samples, block), 1
    )
    count_row = lax.broadcasted_iota(jnp.int32, (2 * samples, lanes), 0)
    cand_hot = jnp.zeros((2 * samples, block), jnp.float32)
    cand_count = jnp.ones((2 * samples, lanes), jnp.float32)
    for side, lengths in enumerate((own_len, sib_len)):
        low = jnp.int32(side * cand_rows)
        for i in range(samples):
            n = lengths[0, i]
            at = side * samples + i
            inside = (row == at) & (token >= low) & (token < low + n)
            cand_hot = jnp.where(inside, 1.0, cand_hot)
            cand_count = jnp.where(count_row == at, n.astype(jnp.float32), cand_count)
            low = low + n
    summed = jnp.dot(
        cand_hot,
        pair,
        precision=lax.Precision.HIGHEST,
        preferred_element_type=jnp.float32,
    )
    val_token = (lax.axis_index("dp") % 2) * half + lax.broadcasted_iota(
        jnp.int32, (half, lanes), 0
    )
    column = lax.broadcasted_iota(jnp.int32, (half, lanes), 1)
    count_column = lax.broadcasted_iota(jnp.int32, (2 * samples, lanes), 1)
    for r in range(ROUNDS):
        val_hot = jnp.zeros((half, lanes), jnp.float32)
        val_count = jnp.ones((2 * samples, lanes), jnp.float32)
        low = jnp.int32(0)
        for j in range(val_len.shape[1]):
            n = val_len[owner[r], j]
            inside = (column == j) & (val_token >= low) & (val_token < low + n)
            val_hot = jnp.where(inside, 1.0, val_hot)
            val_count = jnp.where(count_column == j, n.astype(jnp.float32), val_count)
            low = low + n
        scored = jnp.dot(
            summed[:, r * half : (r + 1) * half],
            val_hot,
            precision=lax.Precision.HIGHEST,
            preferred_element_type=jnp.float32,
        )
        scored = scored * (1.0 / math.sqrt(D * FF)) / jnp.sqrt(cand_count * val_count)
        mine[r] = scored[:samples]
        other[r] = scored[samples:]


def score(cand_rows, own_len, sib_len, val_len, owner, gu_h, x, dy):
    shape = jax.ShapeDtypeStruct((ROUNDS, own_len.shape[1], 128), jnp.float32)
    tiles = list(gu_h) + list(x) + list(dy)
    return pl.pallas_call(
        functools.partial(score_body, len(x), cand_rows),
        in_specs=[IN_SMEM] * 4 + [pl.BlockSpec(memory_space=pltpu.VMEM)] * len(tiles),
        out_shape=[shape, shape],
        compiler_params=pltpu.CompilerParams(vmem_limit_bytes=VMEM),
    )(own_len, sib_len, val_len, owner, *tiles)


def local(
    n_dp,
    n_tensor,
    cand_gate,
    cand_up,
    cand_dh,
    cand_x,
    cand_dy,
    val_gate,
    val_up,
    val_dh,
    val_x,
    val_dy,
    cand_lengths,
    val_lengths,
    round_owner,
):
    chips = n_dp // 2
    ring = list(range(chips // 2)) + list(range(chips - 1, chips // 2 - 1, -1))
    along = []
    for i, chip in enumerate(ring):
        along.append((2 * chip, 2 * ring[(i + 1) % chips]))
        along.append((2 * chip + 1, 2 * ring[(i - 1) % chips] + 1))
    across = [(i, i ^ 1) for i in range(n_dp)]

    core = lax.axis_index("dp") % 2

    cand_rows, val_rows = cand_x.shape[0], val_x.shape[0]
    half = val_rows // 2
    groups, width = cand_gate.shape[1] // FB, cand_x.shape[1]
    count = groups + -(-2 * width // W)
    vals = (val_gate, val_up, val_dh, val_x, val_dy)
    own = (cand_gate, cand_up, cand_dh, cand_x, cand_dy)
    other = (1 - core)[None]

    sib_parts = [None] * count

    def send_half(lo, hi, deps):
        part, mark = pack(other, half, lo, hi - lo, deps, *vals)
        part = lax.ppermute(part, "dp", across)
        for t in range(lo, hi):
            sib_parts[t] = (part, t - lo)
        return mark

    mark = send_half(0, min(2, count), [])
    sib = []

    def send_next(deps):
        array = own[len(sib)]
        array = lax.optimization_barrier((array, *deps))[0]
        sib.append(lax.ppermute(array, "dp", across))

    sib_lengths = lax.ppermute(cand_lengths, "dp", across)

    grams, parts = {}, {}
    steps = count + chips - 1
    held = [[None] * steps for _ in range(ROUNDS)]
    got = [None] * ROUNDS

    def consume(k, deps):
        came = [held[r][k + i] for r in range(ROUNDS) for i in range(chips)]
        kind = slice(0, 3) if k < groups else slice(3, 5)
        mark, done = use(
            k, round_owner, groups, width, chips, n_tensor, own[kind], sib[kind], came, grams, deps
        )
        for name, pieces in done.items():
            parts[name] = [pieces[0]] + [
                lax.ppermute(
                    pieces[m], "tensor", [(z, (z + m) % n_tensor) for z in range(n_tensor)]
                )
                for m in range(1, n_tensor)
            ]
        return mark

    work = []
    cuts = [c for c in (2, 4, 6, 8, 9) if c < count] + [count]
    for lo, hi in zip(cuts[:-1], cuts[1:]):
        work.append((1, functools.partial(send_half, lo, hi)))
    for k in range(count):
        work.append(((k + chips) * ROUNDS - 1, functools.partial(consume, k)))

    def latest(t, r):
        return [held[q][t] if q <= r else held[q][t - 1] for q in range(ROUNDS)]

    slot = 0
    for t in range(steps):
        for r in range(ROUNDS):
            if t < steps - 2:
                part, at = sib_parts[min(t, count - 1)]
                held[r][t] = inject(t, at, r, half, n_dp, round_owner, vals, part, got[r], [mark])
            else:
                held[r][t] = got[r]
            if t < steps - 2:
                got[r] = lax.ppermute(held[r][t], "dp", along)
            elif t == steps - 2:
                last = trim(held[r][t], valid(count - 1 - groups, width), [mark])
                got[r] = lax.ppermute(last, "dp", along)
            if work and work[0][0] <= slot:
                mark = work.pop(0)[1](latest(t, r))
            if slot in (1, 3, 5, 9, 13):
                send_next([mark])
            slot += 1
    while work:
        mark = work.pop(0)[1]([mark])

    mine, theirs = score(
        cand_rows, cand_lengths, sib_lengths, val_lengths, round_owner,
        parts["gu_h"], parts["x"], parts["dy"],
    )
    total = mine + lax.ppermute(theirs, "dp", across)
    turned = [
        lax.ppermute(total, "tensor", [(z, (z + m) % n_tensor) for z in range(n_tensor)])
        for m in range(1, n_tensor)
    ]
    for piece in turned:
        total = total + piece
    return total[:, :, : val_lengths.shape[1]]


def solution(mesh):
    n_dp, n_tensor = mesh.shape["dp"], mesh.shape["tensor"]
    in_specs = (P("dp", "tensor"),) * 10 + (P("dp", None), P(), P())
    return jax.shard_map(
        functools.partial(local, n_dp, n_tensor),
        mesh=mesh,
        in_specs=in_specs,
        out_specs=P(None, "dp", None),
        check_vma=False,
    )
```

```python
import functools
import math

import jax
import jax.numpy as jnp
from jax import lax
from jax.experimental import pallas as pl
from jax.experimental.pallas import tpu as pltpu
from jax.sharding import PartitionSpec as P

D = 8192
FF = 28672
ROUNDS = 2
FB = 896
W = 3 * FB
VMEM = 64 * 1024 * 1024 - 256 * 1024

NT = (((1,), (1,)), ((), ()))


def derive(gate, up, grad_hidden):
    gate_f = gate.astype(jnp.float32)
    up_f = up.astype(jnp.float32)
    grad_f = grad_hidden.astype(jnp.float32)
    sigmoid_gate = jax.nn.sigmoid(gate_f)
    activated = gate_f * sigmoid_gate
    hidden = (activated * up_f).astype(jnp.bfloat16)
    grad_gate = (grad_f * up_f * sigmoid_gate * (1.0 + gate_f * (1.0 - sigmoid_gate))).astype(
        jnp.bfloat16
    )
    grad_up = (grad_f * activated).astype(jnp.bfloat16)
    return (grad_gate, grad_up, hidden)


def segments(j, width):
    out = []
    for which in (0, 1):
        lo = max(j * W, which * width)
        hi = min((j + 1) * W, (which + 1) * width)
        if hi > lo:
            out.append((which, lo - which * width, lo - j * W, hi - lo))
    return out


ANYWHERE = pl.BlockSpec(memory_space=pl.ANY)
IN_HBM = pl.BlockSpec(memory_space=pltpu.HBM)
IN_SMEM = pl.BlockSpec(memory_space=pltpu.SMEM)
MARK = jax.ShapeDtypeStruct((8, 128), jnp.float32)


def place_of(chip, chips):
    return jnp.where(chip < chips // 2, chip, chips // 2 + chips - 1 - chip)


def away_of(me, owner, chips):
    behind = place_of(me // 2, chips) - place_of(owner // 2, chips)
    return lax.rem(jnp.where(me % 2 == 0, behind, -behind) + chips, chips)


def valid(j, width):
    return max(dst + cols for _, _, dst, cols in segments(j, width))


def pack_body(groups, width, first, half, gate, up, dh, x, dy, *rest):
    out = rest[-2]
    k = pl.program_id(0) + first

    @pl.when(k < groups)
    def _():
        out[0, :, 0:FB] = gate[...]
        out[0, :, FB : 2 * FB] = up[...]
        out[0, :, 2 * FB : 3 * FB] = dh[...]

    for j in range(-(-2 * width // W)):

        @pl.when(k == groups + j)
        def _():
            end = 0
            for which, src, dst, cols in segments(j, width):
                out[0, :, dst : dst + cols] = (x, dy)[which][:, src : src + cols]
                end = dst + cols
            if end < W:
                out[0, :, end:W] = jnp.zeros((out.shape[1], W - end), out.dtype)


def pack(half, rows, first, count, deps, *arrays):
    groups, width = arrays[0].shape[1] // FB, arrays[3].shape[1]
    wide = pl.BlockSpec(
        (rows, FB), lambda k, half: (half[0], jnp.minimum(k + first, groups - 1))
    )
    flat = pl.BlockSpec((rows, width), lambda k, half: (half[0], 0))
    return pl.pallas_call(
        functools.partial(pack_body, groups, width, first),
        grid_spec=pltpu.PrefetchScalarGridSpec(
            num_scalar_prefetch=1,
            grid=(count,),
            in_specs=[wide, wide, wide, flat, flat] + [ANYWHERE] * len(deps),
            out_specs=[pl.BlockSpec((1, rows, W), lambda k, half: (k, 0, 0)), IN_HBM],
        ),
        out_shape=[jax.ShapeDtypeStruct((count, rows, W), jnp.bfloat16), MARK],
        cost_estimate=pl.CostEstimate(
            flops=16 * rows * rows * W, bytes_accessed=24 * rows * W, transcendentals=0
        ),
        compiler_params=pltpu.CompilerParams(vmem_limit_bytes=VMEM),
    )(half, *arrays, *deps)


def inject_body(t, at, r, groups, width, n_dp, always, owner, gate, up, dh, x, dy, sib, *rest):
    out, room, sem = rest[-3:]
    rows = out.shape[0]
    if t >= groups + -(-2 * width // W):
        return
    me = lax.axis_index("dp")
    start = pl.multiple_of(me % 2 * rows, rows)
    mine = owner[r] % 2 == me % 2
    first = jnp.logical_or(always, owner[r] // 2 == me // 2)

    if t < groups:
        parts = [(ref, t * FB, i * FB, FB) for i, ref in enumerate((gate, up, dh))]
    else:
        parts = [
            ((x, dy)[which], src, dst, cols)
            for which, src, dst, cols in segments(t - groups, width)
        ]

    def through(sources):
        ins, outs = [], []
        half = rows // 2
        for n in (0, 1):
            some = pl.ds(n * half, half)
            for source, first, src, dst, cols in sources:
                there = room.at[some, pl.ds(dst, cols)]
                i = len(ins)
                here = source.at[pl.ds(first + n * half, half), pl.ds(src, cols)]
                ins.append(pltpu.make_async_copy(here, there, sem.at[0, i]))
                outs.append(
                    pltpu.make_async_copy(there, out.at[some, pl.ds(dst, cols)], sem.at[1, i])
                )
        for copy in ins:
            copy.start()
        for before, copy in zip(ins, outs):
            before.wait()
            copy.start()
        for copy in outs:
            copy.wait()

    @pl.when(first)
    def _():
        @pl.when(mine)
        def _():
            through([(ref, start, src, dst, cols) for ref, src, dst, cols in parts])

        @pl.when(jnp.logical_not(mine))
        def _():
            through([(sib.at[at], 0, dst, dst, cols) for _, _, dst, cols in parts])


def inject(t, at, r, rows, n_dp, owner, vals, sib, held, deps):
    groups, width = vals[0].shape[1] // FB, vals[3].shape[1]
    extra = ([] if held is None else [held]) + list(deps)
    return pl.pallas_call(
        functools.partial(inject_body, t, at, r, groups, width, n_dp, held is None),
        in_specs=[IN_SMEM]
        + [IN_HBM] * (6 if held is None else 7)
        + [ANYWHERE] * len(deps),
        out_specs=IN_HBM,
        out_shape=jax.ShapeDtypeStruct((rows, W), jnp.bfloat16),
        scratch_shapes=[pltpu.VMEM((rows, W), jnp.bfloat16), pltpu.SemaphoreType.DMA((2, 6))],
        input_output_aliases={} if held is None else {7: 0},
        cost_estimate=pl.CostEstimate(
            flops=0, bytes_accessed=4 * rows * W, transcendentals=0
        ),
        compiler_params=pltpu.CompilerParams(vmem_limit_bytes=VMEM),
    )(owner, *vals, sib, *extra)


def trim_body(source, *rest):
    out, room, sem = rest[-3:]
    rows, cols = out.shape
    some = rows // 4
    ins, outs = [], []
    for i in range(4):
        at = pl.ds(i * some, some)
        ins.append(
            pltpu.make_async_copy(source.at[at, pl.ds(0, cols)], room.at[at], sem.at[0, i])
        )
        outs.append(pltpu.make_async_copy(room.at[at], out.at[at], sem.at[1, i]))
    for copy in ins:
        copy.start()
    for before, copy in zip(ins, outs):
        before.wait()
        copy.start()
    for copy in outs:
        copy.wait()


def trim(source, cols, deps):
    rows = source.shape[0]
    return pl.pallas_call(
        trim_body,
        in_specs=[IN_HBM] + [ANYWHERE] * len(deps),
        out_specs=IN_HBM,
        out_shape=jax.ShapeDtypeStruct((rows, cols), source.dtype),
        scratch_shapes=[pltpu.VMEM((rows, cols), source.dtype), pltpu.SemaphoreType.DMA((2, 4))],
        cost_estimate=pl.CostEstimate(flops=0, bytes_accessed=4 * rows * cols, transcendentals=0),
        compiler_params=pltpu.CompilerParams(vmem_limit_bytes=VMEM),
    )(source, *deps)


def use_body(k, groups, width, chips, names, fresh, owner, own, sib, held, accs_in, accs, room, val, sums, sem):
    rows = room.shape[1]
    half = val.shape[0] // ROUNDS
    me = lax.axis_index("dp")
    brought = []
    for r in range(ROUNDS):
        away = away_of(me, owner[r], chips)
        cols = 3 * FB if k < groups else valid(k - groups, width)
        there = val.at[pl.ds(r * half, half), pl.ds(0, cols)]
        for i in range(chips):

            @pl.when(away == i)
            def _():
                pltpu.make_async_copy(
                    held[r * chips + i].at[:, pl.ds(0, cols)], there, sem.at[r]
                ).start()

        brought.append(
            pltpu.make_async_copy(held[r * chips].at[:, pl.ds(0, cols)], there, sem.at[r])
        )
    if k < groups:
        parts = [(i, k * FB, i * FB, FB) for i in range(3)]
    else:
        parts = segments(k - groups, width)
    loads = []
    for side, arrays in enumerate((own, sib)):
        loads.append([])
        for i, (which, src, dst, cols) in enumerate(parts):
            first = 0
            if side == 1 and k < groups:
                first, which = (which % 2) * rows, which // 2
            copy = pltpu.make_async_copy(
                arrays[which].at[pl.ds(first, rows), pl.ds(src, cols)],
                room.at[side, :, pl.ds(dst, cols)],
                sem.at[2 + 3 * side + i],
            )
            copy.start()
            loads[side].append(copy)
    priors, slot = [], 0
    slots = []
    for i, (_, n, _) in enumerate(names):
        slots.append((slot, n))
        if not fresh[i]:
            copy = pltpu.make_async_copy(accs_in.pop(0), sums.at[pl.ds(slot, n)], sem.at[8 + i])
            copy.start()
            priors.append(copy)
        slot += n

    def derive_in(ref):
        def some(i, carry):
            at = [pl.ds(pl.multiple_of(m * FB + i * 128, 128), 128) for m in range(3)]
            new = derive(ref[:, at[0]], ref[:, at[1]], ref[:, at[2]])
            for m in range(3):
                ref[:, at[m]] = new[m]
            return carry

        lax.fori_loop(0, FB // 128, some, 0)

    for copy in brought:
        copy.wait()
    if k < groups:
        derive_in(val)
    for copy in priors:
        copy.wait()
    stores = []
    for side in (0, 1):
        for copy in loads[side]:
            copy.wait()
        at = pl.ds(side * rows, rows)

        def dot(left, right):
            return lax.dot_general(left, right, NT, preferred_element_type=jnp.float32)

        if k < groups:
            derive_in(room.at[side])
            terms = [
                dot(room[side, :, a:b], val[:, a:b]) for a, b in ((0, 2 * FB), (2 * FB, 3 * FB))
            ]
        else:
            terms = [
                dot(room[side, :, dst : dst + cols], val[:, dst : dst + cols])
                for _, _, dst, cols in parts
            ]
        for i, term in enumerate(terms):
            if fresh[i if len(names) > 1 else 0]:
                sums[i, at, :] = term
            else:
                sums[i, at, :] += term
        for i, (_, _, pieces) in enumerate(names):
            if pieces == 0:
                first, n = slots[i]
                copy = pltpu.make_async_copy(
                    sums.at[pl.ds(first, n), at], accs[i][0].at[:, at], sem.at[10 + 2 * side + i]
                )
                copy.start()
                stores.append(copy)
    for i, (_, _, pieces) in enumerate(names):
        first, n = slots[i]
        for m in range(pieces):
            out = accs[i][m]
            block = out.shape[1]
            at = pl.multiple_of(lax.rem(lax.axis_index("tensor") + m, pieces) * block, block)
            out[...] = sums[first : first + n, pl.ds(at, block), :].astype(out.dtype)
    for copy in stores:
        copy.wait()


def use(k, owner, groups, width, chips, n_tensor, own, sib, held, grams, deps):
    cand_rows, half = own[0].shape[0], held[0].shape[0]
    if k < groups:
        names = [("gu_h", 2, n_tensor if k == groups - 1 else 0)]
    else:
        names = [
            (("x", "dy")[which], 1, n_tensor if src + cols == width else 0)
            for which, src, _, cols in segments(k - groups, width)
        ]
    fresh = [name not in grams for name, _, _ in names]
    priors = [grams[name] for name, _, _ in names if name in grams]
    shapes, places, cuts = [], [], []
    for _, n, pieces in names:
        rows = 2 * cand_rows // max(pieces, 1)
        cuts.append(len(shapes))
        for m in range(max(pieces, 1)):
            dtype = jnp.bfloat16 if m else jnp.float32
            shapes.append(jax.ShapeDtypeStruct((n, rows, ROUNDS * half), dtype))
            places.append(pl.BlockSpec(memory_space=pltpu.VMEM) if pieces else IN_HBM)
    cuts.append(len(shapes))
    n_cand, n_held = len(own), len(held)

    def body(owner, *refs):
        a, b = n_cand, n_cand + len(sib)
        c = b + n_held
        d = c + len(priors)
        e = d + len(deps)
        f = e + len(shapes)
        accs = [refs[e + i : e + j] for i, j in zip(cuts[:-1], cuts[1:])]
        use_body(
            k, groups, width, chips, names, fresh, owner, refs[:a], refs[a:b], refs[b:c],
            list(refs[c:d]), accs, *refs[f + 1 :],
        )

    results = pl.pallas_call(
        body,
        in_specs=[IN_SMEM]
        + [IN_HBM] * (n_cand + len(sib) + n_held + len(priors))
        + [ANYWHERE] * len(deps),
        out_specs=places + [IN_HBM],
        out_shape=shapes + [MARK],
        scratch_shapes=[
            pltpu.VMEM((2, cand_rows, W), jnp.bfloat16),
            pltpu.VMEM((ROUNDS * half, W), jnp.bfloat16),
            pltpu.VMEM((2, 2 * cand_rows, ROUNDS * half), jnp.float32),
            pltpu.SemaphoreType.DMA((14,)),
        ],
        cost_estimate=pl.CostEstimate(
            flops=8 * cand_rows * half * W,
            bytes_accessed=4 * (cand_rows + half) * W + 32 * cand_rows * half,
            transcendentals=2 * (cand_rows + half) * FB,
        ),
        compiler_params=pltpu.CompilerParams(vmem_limit_bytes=VMEM),
    )(owner, *own, *sib, *held, *priors, *deps)
    done = {}
    for (name, _, pieces), i, j in zip(names, cuts[:-1], cuts[1:]):
        if pieces:
            done[name] = results[i:j]
        else:
            grams[name] = results[i]
    return results[-1], done


def score_body(pieces, cand_rows, own_len, sib_len, val_len, owner, *refs):
    mine, other = refs[-2:]

    def total(i, slot):
        value = refs[i * pieces][slot]
        for ref in refs[i * pieces + 1 : (i + 1) * pieces]:
            value = value + ref[slot].astype(jnp.float32)
        return value

    pair = total(1, 0) * total(0, 0) + total(0, 1) * total(2, 0)
    block, half = pair.shape[0], pair.shape[1] // ROUNDS
    samples, lanes = own_len.shape[1], mine.shape[2]

    row = lax.broadcasted_iota(jnp.int32, (2 * samples, block), 0)
    token = lax.axis_index("tensor") * block + lax.broadcasted_iota(
        jnp.int32, (2 * samples, block), 1
    )
    count_row = lax.broadcasted_iota(jnp.int32, (2 * samples, lanes), 0)
    cand_hot = jnp.zeros((2 * samples, block), jnp.float32)
    cand_count = jnp.ones((2 * samples, lanes), jnp.float32)
    for side, lengths in enumerate((own_len, sib_len)):
        low = jnp.int32(side * cand_rows)
        for i in range(samples):
            n = lengths[0, i]
            at = side * samples + i
            inside = (row == at) & (token >= low) & (token < low + n)
            cand_hot = jnp.where(inside, 1.0, cand_hot)
            cand_count = jnp.where(count_row == at, n.astype(jnp.float32), cand_count)
            low = low + n
    summed = jnp.dot(
        cand_hot,
        pair,
        precision=lax.Precision.HIGHEST,
        preferred_element_type=jnp.float32,
    )
    val_token = (lax.axis_index("dp") % 2) * half + lax.broadcasted_iota(
        jnp.int32, (half, lanes), 0
    )
    column = lax.broadcasted_iota(jnp.int32, (half, lanes), 1)
    count_column = lax.broadcasted_iota(jnp.int32, (2 * samples, lanes), 1)
    for r in range(ROUNDS):
        val_hot = jnp.zeros((half, lanes), jnp.float32)
        val_count = jnp.ones((2 * samples, lanes), jnp.float32)
        low = jnp.int32(0)
        for j in range(val_len.shape[1]):
            n = val_len[owner[r], j]
            inside = (column == j) & (val_token >= low) & (val_token < low + n)
            val_hot = jnp.where(inside, 1.0, val_hot)
            val_count = jnp.where(count_column == j, n.astype(jnp.float32), val_count)
            low = low + n
        scored = jnp.dot(
            summed[:, r * half : (r + 1) * half],
            val_hot,
            precision=lax.Precision.HIGHEST,
            preferred_element_type=jnp.float32,
        )
        scored = scored * (1.0 / math.sqrt(D * FF)) / jnp.sqrt(cand_count * val_count)
        mine[r] = scored[:samples]
        other[r] = scored[samples:]


def score(cand_rows, own_len, sib_len, val_len, owner, gu_h, x, dy):
    shape = jax.ShapeDtypeStruct((ROUNDS, own_len.shape[1], 128), jnp.float32)
    tiles = list(gu_h) + list(x) + list(dy)
    return pl.pallas_call(
        functools.partial(score_body, len(x), cand_rows),
        in_specs=[IN_SMEM] * 4 + [pl.BlockSpec(memory_space=pltpu.VMEM)] * len(tiles),
        out_shape=[shape, shape],
        compiler_params=pltpu.CompilerParams(vmem_limit_bytes=VMEM),
    )(own_len, sib_len, val_len, owner, *tiles)


def local(
    n_dp,
    n_tensor,
    cand_gate,
    cand_up,
    cand_dh,
    cand_x,
    cand_dy,
    val_gate,
    val_up,
    val_dh,
    val_x,
    val_dy,
    cand_lengths,
    val_lengths,
    round_owner,
):
    chips = n_dp // 2
    ring = list(range(chips // 2)) + list(range(chips - 1, chips // 2 - 1, -1))
    along = []
    for i, chip in enumerate(ring):
        along.append((2 * chip, 2 * ring[(i + 1) % chips]))
        along.append((2 * chip + 1, 2 * ring[(i - 1) % chips] + 1))
    across = [(i, i ^ 1) for i in range(n_dp)]

    core = lax.axis_index("dp") % 2

    cand_rows, val_rows = cand_x.shape[0], val_x.shape[0]
    half = val_rows // 2
    groups, width = cand_gate.shape[1] // FB, cand_x.shape[1]
    count = groups + -(-2 * width // W)
    vals = (val_gate, val_up, val_dh, val_x, val_dy)
    own = (cand_gate, cand_up, cand_dh, cand_x, cand_dy)
    other = (1 - core)[None]

    sib_parts = [None] * count

    def send_half(lo, hi, deps):
        part, mark = pack(other, half, lo, hi - lo, deps, *vals)
        part = lax.ppermute(part, "dp", across)
        for t in range(lo, hi):
            sib_parts[t] = (part, t - lo)
        return mark

    mark = send_half(0, min(2, count), [])
    sib = []

    def send_next(deps):
        arrays = (own[:2], own[2:3], own[3:4], own[4:])[len(sib)]
        arrays = lax.optimization_barrier((*arrays, *deps))[: len(arrays)]
        array = jnp.concatenate(arrays, axis=0) if len(arrays) > 1 else arrays[0]
        sib.append(lax.ppermute(array, "dp", across))

    sib_lengths = lax.ppermute(cand_lengths, "dp", across)

    grams, parts = {}, {}
    steps = count + chips - 1
    held = [[None] * steps for _ in range(ROUNDS)]
    got = [None] * ROUNDS

    def consume(k, deps):
        came = [held[r][k + i] for r in range(ROUNDS) for i in range(chips)]
        kind = slice(0, 3) if k < groups else slice(3, 5)
        mark, done = use(
            k, round_owner, groups, width, chips, n_tensor, own[kind],
            sib[:2] if k < groups else sib[2:4], came, grams, deps
        )
        for name, pieces in done.items():
            parts[name] = [pieces[0]] + [
                lax.ppermute(
                    pieces[m], "tensor", [(z, (z + m) % n_tensor) for z in range(n_tensor)]
                )
                for m in range(1, n_tensor)
            ]
        return mark

    work = []
    cuts = [c for c in (2, 4, 6, 8, 9) if c < count] + [count]
    for lo, hi in zip(cuts[:-1], cuts[1:]):
        work.append((1, functools.partial(send_half, lo, hi)))
    for k in range(count):
        work.append(((k + chips) * ROUNDS - 1, functools.partial(consume, k)))

    def latest(t, r):
        return [held[q][t] if q <= r else held[q][t - 1] for q in range(ROUNDS)]

    slot = 0
    for t in range(steps):
        for r in range(ROUNDS):
            if t < steps - 2:
                part, at = sib_parts[min(t, count - 1)]
                held[r][t] = inject(t, at, r, half, n_dp, round_owner, vals, part, got[r], [mark])
            else:
                held[r][t] = got[r]
            if t < steps - 2:
                got[r] = lax.ppermute(held[r][t], "dp", along)
            elif t == steps - 2:
                last = trim(held[r][t], valid(count - 1 - groups, width), [mark])
                got[r] = lax.ppermute(last, "dp", along)
            if work and work[0][0] <= slot:
                mark = work.pop(0)[1](latest(t, r))
            if slot in (1, 4, 9, 13):
                send_next([mark])
            slot += 1
    while work:
        mark = work.pop(0)[1]([mark])

    mine, theirs = score(
        cand_rows, cand_lengths, sib_lengths, val_lengths, round_owner,
        parts["gu_h"], parts["x"], parts["dy"],
    )
    total = mine + lax.ppermute(theirs, "dp", across)
    turned = [
        lax.ppermute(total, "tensor", [(z, (z + m) % n_tensor) for z in range(n_tensor)])
        for m in range(1, n_tensor)
    ]
    for piece in turned:
        total = total + piece
    return total[:, :, : val_lengths.shape[1]]


def solution(mesh):
    n_dp, n_tensor = mesh.shape["dp"], mesh.shape["tensor"]
    in_specs = (P("dp", "tensor"),) * 10 + (P("dp", None), P(), P())
    return jax.shard_map(
        functools.partial(local, n_dp, n_tensor),
        mesh=mesh,
        in_specs=in_specs,
        out_specs=P(None, "dp", None),
        check_vma=False,
    )
```
